256 devices in a mesh: gx: 32 (over z_lo, x, core), gy: 8 (over y, z_hi).
Axes of the slice: x: 4, y: 4, z: 8 (z_hi: 2, z_lo: 4; z = z_hi * 4 + z_lo), core: 2. Of those that a mesh axis runs over, the one named last changes fastest.
Arguments:
- saved_queries: bfloat16 [128, 64, 16, 128], P('gx', 'gy'), may hold values from -24 to 24
- saved_keys: bfloat16 [4, 128, 64, 16, 128], P(None, 'gx', 'gy'), may hold values from -4.5 to 4.5
- saved_values: bfloat16 [4, 128, 64, 16, 128], P(None, 'gx', 'gy'), may hold values from -4.5 to 4.5
- out_grad: bfloat16 [128, 64, 16, 128], P('gx', 'gy'), may hold values from -4.5 to 4.5
- shifts: int32 [3, 2], replicated, may hold values from -1 to 1, as said below
Outputs:
- d_queries: bfloat16 [128, 64, 16, 128], P('gx', 'gy')
- d_keys: bfloat16 [4, 128, 64, 16, 128], P(None, 'gx', 'gy')
- d_values: bfloat16 [4, 128, 64, 16, 128], P(None, 'gx', 'gy')
The draws below stay inside these ranges and needn't reach their ends.
Inputs may be any that keep to these rules, and one draw needn't show every extreme that they name: `shifts`: at least one entry has magnitude 1.
All inputs are finite; a program needn't handle non-finite values.
Results may differ from the reference program's by a relative error of at most 0.0095.
Values may be sent and summed in bfloat16 or wider, within the bound.
A program may use at most 128 MiB of HBM per device.

```python
import math
import jax
import jax.numpy as jnp
from jax import lax

HEADS = 4
HD = 32
C = 128
FRAMES = 4
PAST = 3
SMAX = 1
REACH = 3
Z = 16
X = 128
Y = 64


def draw_saved_queries(key, part):
    normal_part = jnp.clip(jax.random.normal(jax.random.fold_in(key, 11), (X, Y, Z, C), jnp.float32), -4.5, 4.5)
    return normal_part.astype(jnp.bfloat16)


def draw_saved_keys(key, part):
    normal_part = jnp.clip(jax.random.normal(jax.random.fold_in(key, 12), (FRAMES, X, Y, Z, C), jnp.float32), -4.5, 4.5)
    return normal_part.astype(jnp.bfloat16)


def draw_shifts(key, part):
    offsets_drawn = jax.random.randint(jax.random.fold_in(key, 21), (PAST * 2,), -SMAX, SMAX + 1)
    spot_index = jax.random.randint(jax.random.fold_in(key, 22), (), 0, PAST * 2)
    sign_pick = jax.random.randint(jax.random.fold_in(key, 23), (), 0, 2) * 2 - 1
    flat_offsets = jnp.where(jnp.arange(PAST * 2) == spot_index, sign_pick * SMAX, offsets_drawn)
    return flat_offsets.reshape(PAST, 2).astype(jnp.int32)


def level_of(rng, dims, pieces, low, top_value):
    gain, own = 1.0, jax.random.fold_in(rng, 6)
    for position, shards_of in pieces:
        steps = jnp.exp(jax.random.uniform(jax.random.fold_in(own, position), (shards_of,), jnp.float32, low / len(pieces), top_value / len(pieces)))
        gain = gain * jnp.repeat(steps, dims[position] // shards_of).reshape([-1 if axis == position else 1 for axis in range(len(dims))])
    return gain


def gaussian(own_key, dims, spread, most, shards=(), kind=jnp.bfloat16):
    drawn = spread * jax.random.normal(own_key, dims, jnp.float32)
    if shards:
        drawn = drawn * level_of(own_key, dims, shards, -0.22, 0.18)
    return jnp.clip(drawn, -most, most).astype(kind)


def setup_inputs(seed: int = 0) -> dict:
    key_list = jax.random.split(jax.random.key(seed), 6)
    saved_queries = draw_saved_queries(jax.random.fold_in(key_list[5], 71), 0)
    saved_keys = draw_saved_keys(jax.random.fold_in(key_list[5], 71), 0)
    saved_values = gaussian(key_list[2], (FRAMES, X, Y, Z, C), 1.0, 4.5, ((1, 32), (2, 8)))
    out_grad = gaussian(key_list[3], (X, Y, Z, C), 1.0, 4.5, ((0, 32), (1, 8)))
    shifts = draw_shifts(jax.random.fold_in(key_list[5], 71), 0)
    return dict(saved_queries=saved_queries, saved_keys=saved_keys, saved_values=saved_values, out_grad=out_grad, shifts=shifts)


def neighbour_tiles(step_id, offsets, pad_keys, pad_values):
    frame_id = step_id // 75
    step_x = step_id // 15 % 5
    step_y = step_id // 3 % 5
    step_z = step_id % 3
    shift_x = offsets[frame_id, 0]
    shift_y = offsets[frame_id, 1]
    corner = (frame_id.astype(jnp.int32), (REACH + shift_x - 2 + step_x).astype(jnp.int32), (REACH + shift_y - 2 + step_y).astype(jnp.int32), step_z.astype(jnp.int32), jnp.int32(0))
    key_tile = lax.dynamic_slice(pad_keys, corner, (1, X, Y, Z, C))[0].astype(jnp.float32).reshape(X, Y, Z, HEADS, HD)
    value_tile = lax.dynamic_slice(pad_values, corner, (1, X, Y, Z, C))[0].astype(jnp.float32).reshape(X, Y, Z, HEADS, HD)
    pos_x = jnp.arange(X, dtype=jnp.int32) + shift_x + step_x - 2
    pos_y = jnp.arange(Y, dtype=jnp.int32) + shift_y + step_y - 2
    pos_z = jnp.arange(Z, dtype=jnp.int32) + step_z - 1
    inside_x = (pos_x >= 0) & (pos_x < X)
    inside_y = (pos_y >= 0) & (pos_y < Y)
    inside_z = (pos_z >= 0) & (pos_z < Z)
    in_grid = inside_x[:, None, None] & inside_y[None, :, None] & inside_z[None, None, :]
    return (key_tile, value_tile, in_grid, corner)

def reference(saved_queries, saved_keys, saved_values, out_grad, shifts):
    score_scale = 1.0 / math.sqrt(HD)
    offsets = jnp.concatenate([jnp.zeros((1, 2), jnp.int32), shifts.astype(jnp.int32)], 0)
    widths = ((0, 0), (REACH, REACH), (REACH, REACH), (1, 1), (0, 0))
    pad_keys = jnp.pad(saved_keys, widths)
    pad_values = jnp.pad(saved_values, widths)
    query_f = saved_queries.astype(jnp.float32).reshape(X, Y, Z, HEADS, HD)
    grad_f = out_grad.astype(jnp.float32).reshape(X, Y, Z, HEADS, HD)
    total_steps = FRAMES * 75

    def first_pass(step_id, state_tuple):
        row_max, row_total, row_dot = state_tuple
        key_tile, value_tile, in_grid, corner = neighbour_tiles(step_id, offsets, pad_keys, pad_values)
        scores = lax.optimization_barrier(jnp.sum(query_f * key_tile, -1)) * score_scale
        scores = jnp.where(in_grid[..., None], scores, -1e+30)
        grad_att = lax.optimization_barrier(jnp.sum(grad_f * value_tile, -1))
        new_max = jnp.maximum(row_max, scores)
        rescale = jnp.exp(row_max - new_max)
        exp_scores = jnp.where(in_grid[..., None], jnp.exp(scores - new_max), 0.0)
        return (new_max, row_total * rescale + exp_scores, row_dot * rescale + exp_scores * grad_att)
    start_state = (jnp.full((X, Y, Z, HEADS), -1e+30, jnp.float32), jnp.zeros((X, Y, Z, HEADS), jnp.float32), jnp.zeros((X, Y, Z, HEADS), jnp.float32))
    row_max, row_total, row_dot = lax.fori_loop(0, total_steps, first_pass, start_state)
    row_delta = row_dot / row_total

    def second_pass(step_id, state_tuple):
        grad_q, acc_keys, acc_values = state_tuple
        key_tile, value_tile, in_grid, corner = neighbour_tiles(step_id, offsets, pad_keys, pad_values)
        scores = lax.optimization_barrier(jnp.sum(query_f * key_tile, -1)) * score_scale
        grad_att = lax.optimization_barrier(jnp.sum(grad_f * value_tile, -1))
        attention = jnp.where(in_grid[..., None], jnp.exp(scores - row_max) / row_total, 0.0)
        grad_scores = (attention * (grad_att - row_delta)).astype(jnp.bfloat16)
        grad_scores = lax.optimization_barrier(grad_scores).astype(jnp.float32)
        weights = lax.optimization_barrier(attention.astype(jnp.bfloat16)).astype(jnp.float32)
        grad_q = grad_q + grad_scores[..., None] * key_tile
        key_term = (grad_scores[..., None] * query_f).reshape(X, Y, Z, C)
        value_term = (weights[..., None] * grad_f).reshape(X, Y, Z, C)
        region_k = lax.dynamic_slice(acc_keys, corner, (1, X, Y, Z, C))
        acc_keys = lax.dynamic_update_slice(acc_keys, region_k + key_term[None], corner)
        region_v = lax.dynamic_slice(acc_values, corner, (1, X, Y, Z, C))
        acc_values = lax.dynamic_update_slice(acc_values, region_v + value_term[None], corner)
        return (grad_q, acc_keys, acc_values)
    padded_shape = (FRAMES, X + 2 * REACH, Y + 2 * REACH, Z + 2, C)
    start_grads = (jnp.zeros((X, Y, Z, HEADS, HD), jnp.float32), jnp.zeros(padded_shape, jnp.float32), jnp.zeros(padded_shape, jnp.float32))
    grad_q, acc_keys, acc_values = lax.fori_loop(0, total_steps, second_pass, start_grads)
    d_queries = (grad_q * score_scale).reshape(X, Y, Z, C).astype(jnp.bfloat16)
    d_keys = (acc_keys[:, REACH:REACH + X, REACH:REACH + Y, 1:1 + Z] * score_scale).astype(jnp.bfloat16)
    d_values = acc_values[:, REACH:REACH + X, REACH:REACH + Y, 1:1 + Z].astype(jnp.bfloat16)
    return (d_queries, d_keys, d_values)
```

```python
import functools
import math

import jax
import jax.numpy as jnp
import numpy as np
from jax import lax
from jax.experimental import pallas as pl
from jax.experimental.pallas import tpu as pltpu
from jax.sharding import PartitionSpec as P

HEADS = 4
HD = 32
C = 128
Z = 16
FRAMES = 4
R = 3
BX = 4
BY = 8
HX = BX + 2 * R
HY = BY + 2 * R
SCALE = 1.0 / math.sqrt(HD)
C2 = SCALE * math.log2(math.e)
NEG = -1e30
KEYS_Y = ((0, 2), (0, 4), (0, 6), (2, 8), (4, 8), (6, 8))


def bias_table():
    rx = np.arange(6) - 2
    col = np.arange(4)
    cx, cy = col // 2, col % 2
    okx = np.abs(rx[:, None] - cx[None]) <= 2
    oky = np.abs(rx[:, None] - cy[None]) <= 2
    z = np.arange(Z)
    okz = np.abs(z[:, None] - z[None]) <= 1
    ok = okx[:, None, None, :, None, None] & oky[None, :, None, :, None, None]
    ok = ok & okz[None, None, :, None, None, :]
    ok = np.broadcast_to(ok, (6, 6, Z, 4, HEADS, Z)).reshape(6, 6, Z, 4 * HEADS * Z)
    return jnp.asarray(np.where(ok, 0.0, NEG).astype(np.float32))


def head_masks():
    lane = lax.broadcasted_iota(jnp.int32, (Z, C), 1) // HD
    return [jnp.where(lane == h, 1.0, 0.0).astype(jnp.bfloat16) for h in range(HEADS)]


def expanded(ref, x, y, masks):
    parts = []
    for cx in range(2):
        for cy in range(2):
            column = ref[x + cx, y + cy]
            parts += [column * mask for mask in masks]
    return jnp.concatenate(parts, 0)


def dot_t(a, b):
    return lax.dot_general(a, b, (((1,), (1,)), ((), ())), preferred_element_type=jnp.float32)


def dot_n(a, b):
    return lax.dot_general(a, b, (((1,), (0,)), ((), ())), preferred_element_type=jnp.float32)


def dot_l(a, b):
    return lax.dot_general(a, b, (((0,), (0,)), ((), ())), preferred_element_type=jnp.float32)


def low_half():
    return lax.broadcasted_iota(jnp.int32, (1, C), 1) < C // 2


def blocks(body, f):
    def step(j, carry):
        for by in range(6):
            body(3 * j, 2, 2 * j, by)
        for by in range(6):
            body(1 + j, 4, 0, by)
        return carry

    lax.fori_loop(0, 2, step, 0)


def window_start(shifts_ref, f):
    past = jnp.maximum(f - 1, 0)
    ox = jnp.where(f > 0, shifts_ref[past, 0], 0)
    oy = jnp.where(f > 0, shifts_ref[past, 1], 0)
    return 1 - ox, 1 - oy


def stats_kernel(shifts_ref, q_ref, g_ref, k_ref, v_ref, bias_ref, out_ref, lse_w, dn_w):
    masks = head_masks()
    low = low_half()
    lse_w[...] = jnp.full(lse_w.shape, NEG, jnp.float32)
    dn_w[...] = jnp.zeros(dn_w.shape, jnp.float32)

    def frame(f, carry):
        sx, sy = window_start(shifts_ref, f)

        def body(bx, nx, kx0, by):
            y0, y1 = KEYS_Y[by]
            rows = nx * (y1 - y0) * Z
            qe = expanded(q_ref, sx + 2 * bx, sy + 2 * by, masks)
            ge = expanded(g_ref, sx + 2 * bx, sy + 2 * by, masks)
            kt = k_ref[f, pl.ds(kx0, nx), y0:y1].reshape(rows, C)
            vt = v_ref[f, pl.ds(kx0, nx), y0:y1].reshape(rows, C)
            r0 = y0 + 4 - 2 * by
            bias = bias_ref[pl.ds(kx0 + 4 - 2 * bx, nx), r0 : r0 + y1 - y0].reshape(rows, 256)
            t = (dot_t(kt, qe) + bias).reshape(rows // 8, 8, 256)
            ga = dot_t(vt, ge).reshape(rows // 8, 8, 256)
            m = jnp.max(t, 0)
            e = jnp.exp2((t - m[None]) * C2)
            l = jnp.sum(e, 0)
            d = jnp.sum(e * ga, 0)
            top = jnp.max(m, 0, keepdims=True)
            w = jnp.exp2((m - top) * C2)
            l = jnp.sum(l * w, 0, keepdims=True)
            d = jnp.sum(d * w, 0, keepdims=True)
            lse = top * C2 + jnp.log2(l)
            dn = d / l
            for cx in range(2):
                for val, dst in ((lse, lse_w), (dn, dn_w)):
                    v2 = val[:, cx * C : (cx + 1) * C]
                    other = pltpu.roll(v2, C // 2, 1)
                    dst[f, 2 + 2 * bx + cx, 2 + 2 * by : 3 + 2 * by] = jnp.where(low, v2, other)
                    dst[f, 2 + 2 * bx + cx, 3 + 2 * by : 4 + 2 * by] = jnp.where(low, other, v2)

        blocks(body, f)
        return carry

    lax.fori_loop(0, FRAMES, frame, 0)

    def merge(r, carry):
        ls, ds = [], []
        for f in range(FRAMES):
            sx, sy = window_start(shifts_ref, f)
            ls.append(lse_w[f, r + 2 - sx, pl.ds(2 - sy, 16)])
            ds.append(dn_w[f, r + 2 - sx, pl.ds(2 - sy, 16)])
        top = functools.reduce(jnp.maximum, ls)
        ws = [jnp.exp2(x - top) for x in ls]
        total = sum(ws)
        mean = sum(w * x for w, x in zip(ws, ds)) / total
        out_ref[r] = jnp.where(low, top + jnp.log2(total), mean)
        return carry

    lax.fori_loop(0, HX, merge, 0)


def grads_kernel(
    shifts_ref, q_ref, g_ref, k_ref, v_ref, st_ref, bias_ref, dq_ref, dk_ref, dv_ref, dk_a, dv_a, dq_w
):
    masks = head_masks()
    low = low_half()
    head_of_lane = lax.broadcasted_iota(jnp.int32, (Z, C), 1) // HD
    dq_w[...] = jnp.zeros(dq_w.shape, jnp.float32)

    def frame(f, carry):
        sx, sy = window_start(shifts_ref, f)
        dk_a[...] = jnp.zeros(dk_a.shape, jnp.float32)
        dv_a[...] = jnp.zeros(dv_a.shape, jnp.float32)

        def body(bx, nx, kx0, by):
            y0, y1 = KEYS_Y[by]
            ny = y1 - y0
            rows = nx * ny * Z
            xq, yq = sx + 2 * bx, sy + 2 * by
            qe = expanded(q_ref, xq, yq, masks)
            ge = expanded(g_ref, xq, yq, masks)
            lses, dels = [], []
            for cx in range(2):
                a = st_ref[xq + cx, pl.ds(yq, 1)]
                b = st_ref[xq + cx, pl.ds(yq + 1, 1)]
                lses.append(jnp.where(low, a, pltpu.roll(b, C // 2, 1)))
                dels.append(jnp.where(low, pltpu.roll(a, C // 2, 1), b))
            lse = jnp.concatenate(lses, 1)
            delta = jnp.concatenate(dels, 1)
            kt = k_ref[f, pl.ds(kx0, nx), y0:y1].reshape(rows, C)
            vt = v_ref[f, pl.ds(kx0, nx), y0:y1].reshape(rows, C)
            r0 = y0 + 4 - 2 * by
            bias = bias_ref[pl.ds(kx0 + 4 - 2 * bx, nx), r0 : r0 + ny].reshape(rows, 256)
            att = jnp.exp2((dot_t(kt, qe) + bias) * C2 - lse)
            gs = (att * (dot_t(vt, ge) - delta)).astype(jnp.bfloat16)
            wt = att.astype(jnp.bfloat16)
            dk_a[pl.ds(kx0, nx), y0:y1] += dot_n(gs, qe).reshape(nx, ny, Z, C)
            dv_a[pl.ds(kx0, nx), y0:y1] += dot_n(wt, ge).reshape(nx, ny, Z, C)
            dq = dot_l(gs, kt)
            for cx in range(2):
                for cy in range(2):
                    base = (2 * cx + cy) * HEADS * Z
                    out = dq[base : base + Z]
                    for h in range(1, HEADS):
                        part = dq[base + h * Z : base + (h + 1) * Z]
                        out = jnp.where(head_of_lane == h, part, out)
                    dq_w[f, 2 + 2 * bx + cx, 2 + 2 * by + cy] = out

        blocks(body, f)
        dk_ref[f] = (dk_a[...] * SCALE).astype(jnp.bfloat16)
        dv_ref[f] = dv_a[...].astype(jnp.bfloat16)
        return carry

    lax.fori_loop(0, FRAMES, frame, 0)

    def merge(r, carry):
        total = jnp.zeros((HY, Z, C), jnp.float32)
        for f in range(FRAMES):
            sx, sy = window_start(shifts_ref, f)
            total = total + dq_w[f, r + 2 - sx, pl.ds(2 - sy, HY)]
        dq_ref[r] = total * SCALE
        return carry

    lax.fori_loop(0, HX, merge, 0)


def shifted(block, axis, by):
    n = lax.axis_size(axis)
    pairs = [(i, i + by) for i in range(n) if 0 <= i + by < n]
    return lax.ppermute(block, axis, pairs)


def with_halo(block, axis, dim):
    size = block.shape[dim]
    low = shifted(lax.slice_in_dim(block, size - R, size, axis=dim), axis, 1)
    high = shifted(lax.slice_in_dim(block, 0, R, axis=dim), axis, -1)
    return jnp.concatenate([low, block, high], dim)


def merged_stats(a, b):
    la, lb = a[..., : C // 2], b[..., : C // 2]
    top = jnp.maximum(la, lb)
    wa, wb = jnp.exp2(la - top), jnp.exp2(lb - top)
    total = wa + wb
    mean = (wa * a[..., C // 2 :] + wb * b[..., C // 2 :]) / total
    return jnp.concatenate([top + jnp.log2(total), mean], -1)


def added(block, axis, dim):
    size = block.shape[dim] - 2 * R
    cut = functools.partial(lax.slice_in_dim, block, axis=dim)
    from_next = shifted(cut(0, R).astype(jnp.bfloat16), axis, -1).astype(jnp.float32)
    from_prev = shifted(cut(size + R, size + 2 * R).astype(jnp.bfloat16), axis, 1).astype(jnp.float32)
    own = cut(R, R + size)
    pad_lo, pad_hi = [(0, 0, 0)] * own.ndim, [(0, 0, 0)] * own.ndim
    pad_lo[dim] = (0, size - R, 0)
    pad_hi[dim] = (size - R, 0, 0)
    zero = jnp.float32(0)
    return own + lax.pad(from_prev, zero, pad_lo) + lax.pad(from_next, zero, pad_hi)


def vmem(n):
    return [pl.BlockSpec(memory_space=pltpu.VMEM)] * n


def per_device(saved_queries, saved_keys, saved_values, out_grad, shifts):
    bias = bias_table()
    qg = jnp.stack([saved_queries, out_grad])
    qg = with_halo(with_halo(qg, "gy", 2), "gx", 1)
    q, g = qg[0], qg[1]
    params = pltpu.CompilerParams(vmem_limit_bytes=56 * 2**20)
    smem = [pl.BlockSpec(memory_space=pltpu.SMEM)]
    stats = pl.pallas_call(
        stats_kernel,
        out_shape=jax.ShapeDtypeStruct((HX, 16, C), jnp.float32),
        in_specs=smem + vmem(5),
        out_specs=pl.BlockSpec(memory_space=pltpu.VMEM),
        scratch_shapes=[pltpu.VMEM((FRAMES, 12, 24, C), jnp.float32)] * 2,
        compiler_params=params,
    )(shifts, q, g, saved_keys, saved_values, bias)
    stats = stats[:, :HY]
    absent = jnp.concatenate(
        [jnp.full((C // 2,), NEG, jnp.float32), jnp.zeros((C // 2,), jnp.float32)]
    )
    stats = fold_stats(fold_stats(stats, "gx", 0, absent), "gy", 1, absent)
    stats = with_halo(with_halo(stats, "gy", 1), "gx", 0)
    stats = jnp.pad(stats, ((0, 0), (0, 2), (0, 0)))
    block = jax.ShapeDtypeStruct(saved_keys.shape, jnp.bfloat16)
    dq, dk, dv = pl.pallas_call(
        grads_kernel,
        out_shape=(jax.ShapeDtypeStruct((HX, HY, Z, C), jnp.float32), block, block),
        in_specs=smem + vmem(6),
        out_specs=tuple(vmem(3)),
        scratch_shapes=[
            pltpu.VMEM((BX, BY, Z, C), jnp.float32),
            pltpu.VMEM((BX, BY, Z, C), jnp.float32),
            pltpu.VMEM((FRAMES, 12, 16, Z, C), jnp.float32),
        ],
        compiler_params=params,
    )(shifts, q, g, saved_keys, saved_values, stats, bias)
    dq = added(added(dq, "gx", 0), "gy", 1)
    return dq.astype(jnp.bfloat16), dk, dv


def fold_stats(block, axis, dim, absent):
    size = block.shape[dim] - 2 * R
    me, n = lax.axis_index(axis), lax.axis_size(axis)
    cut = functools.partial(lax.slice_in_dim, block, axis=dim)
    from_next = jnp.where(me < n - 1, shifted(cut(0, R), axis, -1), absent)
    from_prev = jnp.where(me > 0, shifted(cut(size + R, size + 2 * R), axis, 1), absent)
    own = cut(R, R + size)
    shape = list(own.shape)
    shape[dim] = size - R
    rest = jnp.broadcast_to(absent, shape)
    own = merged_stats(own, jnp.concatenate([from_prev, rest], dim))
    return merged_stats(own, jnp.concatenate([rest, from_next], dim))


def solution(mesh):
    block = P("gx", "gy", None, None)
    frames = P(None, "gx", "gy", None, None)
    return jax.shard_map(
        per_device,
        mesh=mesh,
        in_specs=(block, frames, frames, block, P()),
        out_specs=(block, frames, frames),
        check_vma=False,
    )
```

```python
import functools
import math

import jax
import jax.numpy as jnp
import numpy as np
from jax import lax
from jax.experimental import pallas as pl
from jax.experimental.pallas import tpu as pltpu
from jax.sharding import PartitionSpec as P

HEADS = 4
HD = 32
C = 128
Z = 16
FRAMES = 4
R = 3
BX = 4
BY = 8
HX = BX + 2 * R
HY = BY + 2 * R
SCALE = 1.0 / math.sqrt(HD)
C2 = SCALE * math.log2(math.e)
NEG = -1e30
KEYS_Y = ((0, 2), (0, 4), (0, 6), (2, 8), (4, 8), (6, 8))


def bias_table():
    rx = np.arange(6) - 2
    col = np.arange(4)
    cx, cy = col // 2, col % 2
    okx = np.abs(rx[:, None] - cx[None]) <= 2
    oky = np.abs(rx[:, None] - cy[None]) <= 2
    z = np.arange(Z)
    okz = np.abs(z[:, None] - z[None]) <= 1
    ok = okx[:, None, None, :, None, None] & oky[None, :, None, :, None, None]
    ok = ok & okz[None, None, :, None, None, :]
    ok = np.broadcast_to(ok, (6, 6, Z, 4, HEADS, Z)).reshape(6, 6, Z, 4 * HEADS * Z)
    return jnp.asarray(np.where(ok, 0.0, NEG).astype(np.float32))


def head_masks():
    lane = lax.broadcasted_iota(jnp.int32, (Z, C), 1) // HD
    return [jnp.where(lane == h, 1.0, 0.0).astype(jnp.bfloat16) for h in range(HEADS)]


def expanded(ref, which, x, y, masks):
    parts = []
    for cx in range(2):
        for cy in range(2):
            column = ref[which, x + cx, y + cy]
            parts += [column * mask for mask in masks]
    return jnp.concatenate(parts, 0)


def dot_t(a, b):
    return lax.dot_general(a, b, (((1,), (1,)), ((), ())), preferred_element_type=jnp.float32)


def dot_n(a, b):
    return lax.dot_general(a, b, (((1,), (0,)), ((), ())), preferred_element_type=jnp.float32)


def dot_l(a, b):
    return lax.dot_general(a, b, (((0,), (0,)), ((), ())), preferred_element_type=jnp.float32)


def low_half():
    return lax.broadcasted_iota(jnp.int32, (1, C), 1) < C // 2


def window_start(shifts_ref, f):
    past = jnp.maximum(f - 1, 0)
    ox = jnp.where(f > 0, shifts_ref[past, 0], 0)
    oy = jnp.where(f > 0, shifts_ref[past, 1], 0)
    return 1 - ox, 1 - oy


def merged(a, b):
    low = lax.broadcasted_iota(jnp.int32, a.shape, a.ndim - 1) < C // 2
    la = jnp.where(low, a, pltpu.roll(a, C // 2, a.ndim - 1))
    lb = jnp.where(low, b, pltpu.roll(b, C // 2, b.ndim - 1))
    top = jnp.maximum(la, lb)
    wa, wb = jnp.exp2(la - top), jnp.exp2(lb - top)
    total = wa + wb
    return jnp.where(low, top + jnp.log2(total), (wa * a + wb * b) / total)


class Exchange:
    def __init__(self, axis, index, sems, forward, backward):
        me, n = lax.axis_index(axis), lax.axis_size(axis)
        send, recv = sems
        self.has_next, self.has_prev = me < n - 1, me > 0
        self.forward = [
            self.copy(src, dst, send.at[index + i], recv.at[index + i], {axis: me + 1})
            for i, (src, dst) in enumerate(forward)
        ]
        index += len(forward)
        self.backward = [
            self.copy(src, dst, send.at[index + i], recv.at[index + i], {axis: me - 1})
            for i, (src, dst) in enumerate(backward)
        ]

    @staticmethod
    def copy(src, dst, send, recv, device):
        return pltpu.make_async_remote_copy(
            src_ref=src,
            dst_ref=dst,
            send_sem=send,
            recv_sem=recv,
            device_id=device,
            device_id_type=pl.DeviceIdType.MESH,
        )

    def start(self):
        @pl.when(self.has_next)
        def _():
            for c in self.forward:
                c.start()

        @pl.when(self.has_prev)
        def _():
            for c in self.backward:
                c.start()

    def wait_recv(self):
        @pl.when(self.has_prev)
        def _():
            for c in self.forward:
                c.wait_recv()

        @pl.when(self.has_next)
        def _():
            for c in self.backward:
                c.wait_recv()

    def wait_send(self):
        @pl.when(self.has_next)
        def _():
            for c in self.forward:
                c.wait_send()

        @pl.when(self.has_prev)
        def _():
            for c in self.backward:
                c.wait_send()


MID = (2, 3)
OUTER = (0, 1, 4, 5)


def kernel(
    shifts_ref, q_in, g_in, k_in, v_in, bias_in, dq_ref, dk_ref, dv_ref,
    k_ref, v_ref, bias_ref, qgx, qgy, qgh, lse_w, dn_w, sys_, syr, ownc, sxr, finx, finy, fin,
    dk_a, dv_a, dq_w, dys, dyr, own_dq, dxs, dxr, local_sem, send_sem, recv_sem,
):
    sems = (send_sem, recv_sem)
    masks = head_masks()
    low = low_half()
    head_of_lane = lax.broadcasted_iota(jnp.int32, (Z, C), 1) // HD
    loads = [
        pltpu.make_async_copy(src, dst, local_sem.at[i])
        for i, (src, dst) in enumerate(
            (
                (q_in, qgx.at[0, R : R + BX]),
                (g_in, qgx.at[1, R : R + BX]),
                (k_in, k_ref),
                (v_in, v_ref),
                (bias_in, bias_ref),
            )
        )
    ]
    for c in loads:
        c.start()

    zero16 = jnp.bfloat16(0)
    neutral = jnp.where(low, NEG, 0.0)
    for ref in (qgx.at[:, 0:R], qgx.at[:, R + BX : HX], qgy, dyr, dxr):
        ref[...] = jnp.full(ref.shape, zero16)
    for ref in (syr, sxr):
        ref[...] = jnp.broadcast_to(neutral, ref.shape)
    for ref in (finx, finy):
        ref[...] = jnp.zeros(ref.shape, jnp.float32)

    barrier = pltpu.get_barrier_semaphore()
    for axis in ("gx", "gy"):
        me, n = lax.axis_index(axis), lax.axis_size(axis)
        for there, step in ((me > 0, -1), (me < n - 1, 1)):

            @pl.when(there)
            def _():
                pl.semaphore_signal(
                    barrier, inc=1, device_id={axis: me + step}, device_id_type=pl.DeviceIdType.MESH
                )

    peers = jnp.int32(0)
    for axis in ("gx", "gy"):
        me, n = lax.axis_index(axis), lax.axis_size(axis)
        peers = peers + jnp.where(me > 0, 1, 0) + jnp.where(me < n - 1, 1, 0)
    pl.semaphore_wait(barrier, peers)

    tail = slice(BX - R, BX)
    halo_y = Exchange(
        "gy", 0, sems,
        [(q_in.at[:, BY - R : BY], qgy.at[0, 0, R : R + BX]), (g_in.at[:, BY - R : BY], qgy.at[0, 1, R : R + BX])],
        [(q_in.at[:, 0:R], qgy.at[1, 0, R : R + BX]), (g_in.at[:, 0:R], qgy.at[1, 1, R : R + BX])],
    )
    halo_x = Exchange(
        "gx", 4, sems,
        [(q_in.at[tail], qgx.at[0, 0:R]), (g_in.at[tail], qgx.at[1, 0:R])],
        [(q_in.at[0:R], qgx.at[0, R + BX : HX]), (g_in.at[0:R], qgx.at[1, R + BX : HX])],
    )
    halo_c = Exchange(
        "gx", 8, sems,
        [(qgy.at[:, :, BX : BX + R], qgy.at[:, :, 0:R])],
        [(qgy.at[:, :, R : 2 * R], qgy.at[:, :, R + BX : HX])],
    )
    stat_y = Exchange("gy", 10, sems, [(sys_.at[1], syr.at[0])], [(sys_.at[0], syr.at[1])])
    stat_x = Exchange(
        "gx", 12, sems, [(ownc.at[R + BX : HX], sxr.at[0])], [(ownc.at[0:R], sxr.at[1])]
    )
    fin_y = Exchange(
        "gy", 14, sems,
        [(finx.at[R : R + BX], finy.at[0, R : R + BX])],
        [(finx.at[R : R + BX], finy.at[1, R : R + BX])],
    )
    fin_x = Exchange(
        "gx", 16, sems,
        [(finx.at[BX : BX + R], finx.at[0:R])],
        [(finx.at[R : 2 * R], finx.at[R + BX : HX])],
    )
    fin_c = Exchange(
        "gx", 18, sems,
        [(finy.at[:, BX : BX + R], finy.at[:, 0:R])],
        [(finy.at[:, R : 2 * R], finy.at[:, R + BX : HX])],
    )
    dq_y = Exchange("gy", 20, sems, [(dys.at[1], dyr.at[0])], [(dys.at[0], dyr.at[1])])
    dq_x = Exchange("gx", 22, sems, [(dxs.at[1], dxr.at[0])], [(dxs.at[0], dxr.at[1])])

    halo_y.start()
    halo_x.start()
    lse_w[...] = jnp.full(lse_w.shape, NEG, jnp.float32)
    dn_w[...] = jnp.zeros(dn_w.shape, jnp.float32)
    dk_a[...] = jnp.zeros(dk_a.shape, jnp.float32)
    dv_a[...] = jnp.zeros(dv_a.shape, jnp.float32)
    dq_w[...] = jnp.zeros(dq_w.shape, jnp.float32)

    def part(body, bys, first, last, hook=None):
        def frame(f, carry):
            if hook is not None:
                pl.when(f == last - 1)(hook)
            sx, sy = window_start(shifts_ref, f)

            def step(j, carry):
                for by in bys:
                    body(f, sx, sy, 3 * j, 2, 2 * j, by)
                for by in bys:
                    body(f, sx, sy, 1 + j, 4, 0, by)
                return carry

            lax.fori_loop(0, 2, step, 0)
            return carry

        lax.fori_loop(first, last, frame, 0)

    def operands(f, sx, sy, bx, nx, kx0, by):
        y0, y1 = KEYS_Y[by]
        rows = nx * (y1 - y0) * Z
        xq, yq = sx + 2 * bx, sy + 2 * by
        src, yo = (qgx, yq - R) if by in MID else (qgh, yq)
        qe = expanded(src, 0, xq, yo, masks)
        ge = expanded(src, 1, xq, yo, masks)
        kt = k_ref[f, pl.ds(kx0, nx), y0:y1].reshape(rows, C)
        vt = v_ref[f, pl.ds(kx0, nx), y0:y1].reshape(rows, C)
        r0 = y0 + 4 - 2 * by
        bias = bias_ref[pl.ds(kx0 + 4 - 2 * bx, nx), r0 : r0 + y1 - y0].reshape(rows, 256)
        return qe, ge, kt, vt, bias, rows

    def stats(f, sx, sy, bx, nx, kx0, by):
        qe, ge, kt, vt, bias, rows = operands(f, sx, sy, bx, nx, kx0, by)
        t = (dot_t(kt, qe) + bias).reshape(rows // 8, 8, 256)
        ga = dot_t(vt, ge).reshape(rows // 8, 8, 256)
        m = jnp.max(t, 0)
        e = jnp.exp2((t - m[None]) * C2)
        l = jnp.sum(e, 0)
        d = jnp.sum(e * ga, 0)
        top = jnp.max(m, 0, keepdims=True)
        w = jnp.exp2((m - top) * C2)
        l = jnp.sum(l * w, 0, keepdims=True)
        d = jnp.sum(d * w, 0, keepdims=True)
        lse = top * C2 + jnp.log2(l)
        dn = d / l
        for cx in range(2):
            for val, dst in ((lse, lse_w), (dn, dn_w)):
                v2 = val[:, cx * C : (cx + 1) * C]
                other = pltpu.roll(v2, C // 2, 1)
                dst[f, 2 + 2 * bx + cx, 2 + 2 * by : 3 + 2 * by] = jnp.where(low, v2, other)
                dst[f, 2 + 2 * bx + cx, 3 + 2 * by : 4 + 2 * by] = jnp.where(low, other, v2)

    def grads(f, sx, sy, bx, nx, kx0, by):
        qe, ge, kt, vt, bias, rows = operands(f, sx, sy, bx, nx, kx0, by)
        y0, y1 = KEYS_Y[by]
        xq, yq = sx + 2 * bx, sy + 2 * by
        src, yo = (finx, yq - R) if by in MID else (fin, yq + 5)
        lses, dels = [], []
        for cx in range(2):
            a = src[xq + cx, pl.ds(yo, 1)]
            b = src[xq + cx, pl.ds(yo + 1, 1)]
            lses.append(jnp.where(low, a, pltpu.roll(b, C // 2, 1)))
            dels.append(jnp.where(low, pltpu.roll(a, C // 2, 1), b))
        lse = jnp.concatenate(lses, 1)
        delta = jnp.concatenate(dels, 1)
        att = jnp.exp2((dot_t(kt, qe) + bias) * C2 - lse)
        gs = (att * (dot_t(vt, ge) - delta)).astype(jnp.bfloat16)
        wt = att.astype(jnp.bfloat16)
        dk_a[f, pl.ds(kx0, nx), y0:y1] += dot_n(gs, qe).reshape(nx, y1 - y0, Z, C)
        dv_a[f, pl.ds(kx0, nx), y0:y1] += dot_n(wt, ge).reshape(nx, y1 - y0, Z, C)
        dq = dot_l(gs, kt)
        for cx in range(2):
            for cy in range(2):
                base = (2 * cx + cy) * HEADS * Z
                out = dq[base : base + Z]
                for h in range(1, HEADS):
                    piece = dq[base + h * Z : base + (h + 1) * Z]
                    out = jnp.where(head_of_lane == h, piece, out)
                dq_w[f, 2 + 2 * bx + cx, 2 + 2 * by + cy] = out

    def frames_merged(r):
        ls, ds = [], []
        for f in range(FRAMES):
            sx, sy = window_start(shifts_ref, f)
            ls.append(lse_w[f, r + 2 - sx, pl.ds(2 - sy, 16)])
            ds.append(dn_w[f, r + 2 - sx, pl.ds(2 - sy, 16)])
        top = functools.reduce(jnp.maximum, ls)
        ws = [jnp.exp2(x - top) for x in ls]
        total = sum(ws)
        mean = sum(w * x for w, x in zip(ws, ds)) / total
        return jnp.where(low, top + jnp.log2(total), mean)

    halo_x.wait_recv()
    for c in loads:
        c.wait()

    def forward_corners():
        halo_y.wait_recv()
        halo_c.start()

    part(stats, MID, 0, 2, forward_corners)
    halo_c.wait_recv()

    def assemble(r, carry):
        for a in range(2):
            qgh[a, r, 0:R] = qgy[0, a, r]
            qgh[a, r, R : R + BY] = qgx[a, r]
            qgh[a, r, R + BY : HY] = qgy[1, a, r]
        return carry

    lax.fori_loop(0, HX, assemble, 0)
    part(stats, OUTER, 0, 4)
    row8 = lax.broadcasted_iota(jnp.int32, (8, C), 0)

    def rims(r, carry):
        val = frames_merged(r)
        sys_[0, r] = jnp.where(row8 >= 8 - R, pltpu.roll(val[0:8], 8 - R, 0), neutral)
        sys_[1, r] = jnp.where(row8 < R, pltpu.roll(val[8:16], 8 - R, 0), neutral)
        return carry

    lax.fori_loop(0, HX, rims, 0)
    stat_y.start()
    part(stats, MID, 2, 4)
    stat_y.wait_recv()

    def core_rows(r, carry):
        ownc[r] = merged(merged(frames_merged(r)[R : R + BY], syr[0, r]), syr[1, r])
        return carry

    lax.fori_loop(0, HX, core_rows, 0)
    stat_x.start()
    stat_x.wait_recv()
    for i in range(BX):
        val = ownc[R + i]
        if i < R:
            val = merged(val, sxr[0, i])
        if i >= BX - R:
            val = merged(val, sxr[1, i - (BX - R)])
        finx[R + i] = val
    fin_y.start()
    fin_x.start()

    fin_x.wait_recv()

    def forward_stats():
        fin_y.wait_recv()
        fin_c.start()

    part(grads, MID, 0, 2, forward_stats)
    fin_c.wait_recv()
    fin[:, 0:8] = finy[0]
    fin[:, 8:16] = finx[...]
    fin[:, 16:24] = finy[1]
    part(grads, OUTER, 0, 4)

    def dq_rims(r, carry):
        for side, at in ((0, 0), (1, R + BY)):
            total = jnp.zeros((R, Z, C), jnp.float32)
            for f in range(FRAMES):
                sx, sy = window_start(shifts_ref, f)
                total = total + dq_w[f, r + 2 - sx, pl.ds(2 - sy + at, R)]
            dys[side, r] = (total * SCALE).astype(jnp.bfloat16)
        return carry

    lax.fori_loop(0, HX, dq_rims, 0)
    dq_y.start()
    part(grads, MID, 2, 4)
    dq_y.wait_recv()

    def dq_core(r, carry):
        total = jnp.zeros((BY, Z, C), jnp.float32)
        for f in range(FRAMES):
            sx, sy = window_start(shifts_ref, f)
            total = total + dq_w[f, r + 2 - sx, pl.ds(2 - sy + R, BY)]
        own_dq[r] = total * SCALE
        own_dq[r, 0:R] += dyr[0, r].astype(jnp.float32)
        own_dq[r, BY - R : BY] += dyr[1, r].astype(jnp.float32)
        return carry

    lax.fori_loop(0, HX, dq_core, 0)
    dxs[0] = own_dq[0:R].astype(jnp.bfloat16)
    dxs[1] = own_dq[R + BX : HX].astype(jnp.bfloat16)
    dq_x.start()

    def convert(f, carry):
        dk_ref[f] = (dk_a[f] * SCALE).astype(jnp.bfloat16)
        dv_ref[f] = dv_a[f].astype(jnp.bfloat16)
        return carry

    lax.fori_loop(0, FRAMES, convert, 0)
    dq_x.wait_recv()
    for i in range(BX):
        val = own_dq[R + i]
        if i < R:
            val = val + dxr[0, i].astype(jnp.float32)
        if i >= BX - R:
            val = val + dxr[1, i - (BX - R)].astype(jnp.float32)
        dq_ref[i] = val.astype(jnp.bfloat16)
    for ex in (halo_y, halo_x, halo_c, stat_y, stat_x, fin_y, fin_x, fin_c, dq_y, dq_x):
        ex.wait_send()


def per_device(saved_queries, saved_keys, saved_values, out_grad, shifts):
    bf, f32 = jnp.bfloat16, jnp.float32
    frames = saved_keys.shape
    vmem = pl.BlockSpec(memory_space=pltpu.VMEM)
    return pl.pallas_call(
        kernel,
        out_shape=(
            jax.ShapeDtypeStruct(saved_queries.shape, bf),
            jax.ShapeDtypeStruct(frames, bf),
            jax.ShapeDtypeStruct(frames, bf),
        ),
        in_specs=[pl.BlockSpec(memory_space=pltpu.SMEM)] + [pl.BlockSpec(memory_space=pl.ANY)] * 5,
        out_specs=(vmem, vmem, vmem),
        scratch_shapes=[
            pltpu.VMEM(frames, bf),
            pltpu.VMEM(frames, bf),
            pltpu.VMEM((6, 6, Z, 256), f32),
            pltpu.VMEM((2, HX, BY, Z, C), bf),
            pltpu.VMEM((2, 2, HX, R, Z, C), bf),
            pltpu.VMEM((2, HX, HY, Z, C), bf),
            pltpu.VMEM((FRAMES, 12, 24, C), f32),
            pltpu.VMEM((FRAMES, 12, 24, C), f32),
            pltpu.VMEM((2, HX, 8, C), f32),
            pltpu.VMEM((2, HX, 8, C), f32),
            pltpu.VMEM((HX, 8, C), f32),
            pltpu.VMEM((2, R, 8, C), f32),
            pltpu.VMEM((HX, 8, C), f32),
            pltpu.VMEM((2, HX, 8, C), f32),
            pltpu.VMEM((HX, 24, C), f32),
            pltpu.VMEM(frames, f32),
            pltpu.VMEM(frames, f32),
            pltpu.VMEM((FRAMES, 12, 16, Z, C), f32),
            pltpu.VMEM((2, HX, R, Z, C), bf),
            pltpu.VMEM((2, HX, R, Z, C), bf),
            pltpu.VMEM((HX, BY, Z, C), f32),
            pltpu.VMEM((2, R, BY, Z, C), bf),
            pltpu.VMEM((2, R, BY, Z, C), bf),
            pltpu.SemaphoreType.DMA((5,)),
            pltpu.SemaphoreType.DMA((24,)),
            pltpu.SemaphoreType.DMA((24,)),
        ],
        compiler_params=pltpu.CompilerParams(
            collective_id=0, has_side_effects=True, vmem_limit_bytes=60 * 2**20
        ),
    )(shifts, saved_queries, out_grad, saved_keys, saved_values, bias_table())


def solution(mesh):
    block = P("gx", "gy", None, None)
    frames = P(None, "gx", "gy", None, None)
    return jax.shard_map(
        per_device,
        mesh=mesh,
        in_specs=(block, frames, frames, block, P()),
        out_specs=(block, frames, frames),
        check_vma=False,
    )
```

```python
import functools
import math

import jax
import jax.numpy as jnp
import numpy as np
from jax import lax
from jax.experimental import pallas as pl
from jax.experimental.pallas import tpu as pltpu
from jax.sharding import PartitionSpec as P

HEADS = 4
HD = 32
C = 128
Z = 16
FRAMES = 4
R = 3
BX = 4
BY = 8
HX = BX + 2 * R
HY = BY + 2 * R
SCALE = 1.0 / math.sqrt(HD)
C2 = SCALE * math.log2(math.e)
NEG = -1e30
KEYS_Y = ((0, 2), (0, 4), (0, 6), (2, 8), (4, 8), (6, 8))


def bias_table():
    rx = np.arange(6) - 2
    col = np.arange(4)
    cx, cy = col // 2, col % 2
    okx = np.abs(rx[:, None] - cx[None]) <= 2
    oky = np.abs(rx[:, None] - cy[None]) <= 2
    z = np.arange(Z)
    okz = np.abs(z[:, None] - z[None]) <= 1
    ok = okx[:, None, None, :, None, None] & oky[None, :, None, :, None, None]
    ok = ok & okz[None, None, :, None, None, :]
    ok = np.broadcast_to(ok, (6, 6, Z, 4, HEADS, Z)).reshape(6, 6, Z, 4 * HEADS * Z)
    return jnp.asarray(np.where(ok, 0.0, NEG).astype(np.float32))


def head_masks():
    lane = lax.broadcasted_iota(jnp.int32, (Z, C), 1) // HD
    return [jnp.where(lane == h, 1.0, 0.0).astype(jnp.bfloat16) for h in range(HEADS)]


def expanded(ref, which, x, y, masks):
    parts = []
    for cx in range(2):
        for cy in range(2):
            column = ref[which, x + cx, y + cy]
            parts += [column * mask for mask in masks]
    return jnp.concatenate(parts, 0)


def dot_t(a, b):
    return lax.dot_general(a, b, (((1,), (1,)), ((), ())), preferred_element_type=jnp.float32)


def dot_n(a, b):
    return lax.dot_general(a, b, (((1,), (0,)), ((), ())), preferred_element_type=jnp.float32)


def dot_l(a, b):
    return lax.dot_general(a, b, (((0,), (0,)), ((), ())), preferred_element_type=jnp.float32)


def low_half():
    return lax.broadcasted_iota(jnp.int32, (1, C), 1) < C // 2


def window_start(shifts_ref, f):
    past = jnp.maximum(f - 1, 0)
    ox = jnp.where(f > 0, shifts_ref[past, 0], 0)
    oy = jnp.where(f > 0, shifts_ref[past, 1], 0)
    return 1 - ox, 1 - oy


def merged(a, b):
    low = lax.broadcasted_iota(jnp.int32, a.shape, a.ndim - 1) < C // 2
    la = jnp.where(low, a, pltpu.roll(a, C // 2, a.ndim - 1))
    lb = jnp.where(low, b, pltpu.roll(b, C // 2, b.ndim - 1))
    top = jnp.maximum(la, lb)
    wa, wb = jnp.exp2(la - top), jnp.exp2(lb - top)
    total = wa + wb
    return jnp.where(low, top + jnp.log2(total), (wa * a + wb * b) / total)


class Message:
    def __init__(self, offset, src, dst, index, sems):
        device, self.has_target, self.has_source = {}, True, True
        for axis, by in offset.items():
            at, n = lax.axis_index(axis), lax.axis_size(axis)
            device[axis] = at + by
            to, back = at + by, at - by
            self.has_target = self.has_target & (to >= 0) & (to < n)
            self.has_source = self.has_source & (back >= 0) & (back < n)
        self.copy = pltpu.make_async_remote_copy(
            src_ref=src,
            dst_ref=dst,
            send_sem=sems[0].at[index],
            recv_sem=sems[1].at[index],
            device_id=device,
            device_id_type=pl.DeviceIdType.MESH,
        )

    def start(self):
        pl.when(self.has_target)(self.copy.start)

    def wait_recv(self):
        pl.when(self.has_source)(self.copy.wait_recv)

    def wait_send(self):
        pl.when(self.has_target)(self.copy.wait_send)


PEERS = tuple(
    [{"gx": d} for d in (-2, -1, 1, 2)]
    + [{"gy": d} for d in (-1, 1)]
    + [{"gx": dx, "gy": dy} for dx in (-1, 1) for dy in (-1, 1)]
)
MID = (2, 3)
OUTER = (0, 1, 4, 5)
NROWS = [2 * Z * (b - a) for a, b in KEYS_Y]
FIRST_ROW = {2: [sum(NROWS[:i]) for i in range(6)]}
FIRST_ROW[4] = [sum(NROWS) + 2 * v for v in FIRST_ROW[2]]
ROWS = 3 * sum(NROWS)
MESSAGES = 32


def kernel(
    shifts_in, q_in, g_in, k_in, v_in, bias_in, dq_out, dk_out, dv_out,
    shifts_ref, k_ref, v_ref, bias_ref, qgx, qgy, qgh, lse_w, dn_w, part_s, ry, rx1, rx2, fin,
    e_s, ga_s, m_s, dk_a, dv_a, dq_w, dys, dyr, dcr, own_dq, dxs, dxr, dq_v,
    local_sem, out_sem, send_sem, recv_sem,
):
    sems = (send_sem, recv_sem)
    masks = head_masks()
    low = low_half()
    head_of_lane = lax.broadcasted_iota(jnp.int32, (Z, C), 1) // HD
    loads = [
        pltpu.make_async_copy(src, dst, local_sem.at[i])
        for i, (src, dst) in enumerate(
            (
                (shifts_in, shifts_ref),
                (q_in, qgx.at[0, R : R + BX]),
                (g_in, qgx.at[1, R : R + BX]),
                (k_in, k_ref),
                (v_in, v_ref),
                (bias_in, bias_ref),
            )
        )
    ]
    for c in loads:
        c.start()

    zero16 = jnp.bfloat16(0)
    neutral = jnp.where(low, NEG, 0.0)
    for ref in (qgx.at[:, 0:R], qgx.at[:, R + BX : HX], qgy, dyr, dcr, dxr):
        ref[...] = jnp.full(ref.shape, zero16)
    for ref in (ry, rx1, rx2):
        ref[...] = jnp.broadcast_to(neutral, ref.shape)

    barrier = pltpu.get_barrier_semaphore()
    count = jnp.int32(0)
    for offset in PEERS:
        there = True
        for axis, by in offset.items():
            to = lax.axis_index(axis) + by
            there = there & (to >= 0) & (to < lax.axis_size(axis))
        device = {axis: lax.axis_index(axis) + by for axis, by in offset.items()}
        count = count + jnp.where(there, 1, 0)

        @pl.when(there)
        def _():
            pl.semaphore_signal(barrier, inc=1, device_id=device, device_id_type=pl.DeviceIdType.MESH)

    pl.semaphore_wait(barrier, count)

    made = []

    def message(offset, src, dst):
        made.append(Message(offset, src, dst, len(made), sems))
        return made[-1]

    up, down, right, left = {"gy": 1}, {"gy": -1}, {"gx": 1}, {"gx": -1}
    tail = slice(BX - R, BX)
    own = slice(R, R + BX)
    past = slice(R + BX, HX)
    halo_y, halo_x = [], []
    for i, ref in enumerate((q_in, g_in)):
        halo_y.append(message(up, ref.at[:, BY - R : BY], qgy.at[0, i, own]))
        halo_y.append(message(down, ref.at[:, 0:R], qgy.at[1, i, own]))
        halo_x.append(message(right, ref.at[tail], qgx.at[i, 0:R]))
        halo_x.append(message(left, ref.at[0:R], qgx.at[i, past]))
    halo_c = [
        message(right, qgy.at[:, :, BX : BX + R], qgy.at[:, :, 0:R]),
        message(left, qgy.at[:, :, R : 2 * R], qgy.at[:, :, past]),
    ]
    stat_y = [
        message(up, part_s.at[0, :, 8:16], ry.at[0]),
        message(down, part_s.at[0, :, 0:8], ry.at[1]),
    ]
    stat_x = [
        message(right, part_s.at[1, 4:10], rx1.at[0]),
        message(left, part_s.at[1, 0:6], rx1.at[1]),
        message({"gx": 2}, part_s.at[1, 8:10], rx2.at[0]),
        message({"gx": -2}, part_s.at[1, 0:2], rx2.at[1]),
    ]
    dq_far = [
        message(up, dys.at[1, own], dyr.at[0]),
        message(down, dys.at[0, own], dyr.at[1]),
    ]
    for xs, dx, rows in ((0, 1, past), (1, -1, slice(0, R))):
        for ys, dy, side in ((0, 1, 1), (1, -1, 0)):
            dq_far.append(message({"gx": dx, "gy": dy}, dys.at[side, rows], dcr.at[xs, ys]))
    dq_near = [message(right, dxs.at[1], dxr.at[0]), message(left, dxs.at[0], dxr.at[1])]

    for m in halo_y + halo_x:
        m.start()
    lse_w[...] = jnp.full(lse_w.shape, NEG, jnp.float32)
    dn_w[...] = jnp.zeros(dn_w.shape, jnp.float32)
    dk_a[...] = jnp.zeros(dk_a.shape, jnp.float32)
    dv_a[...] = jnp.zeros(dv_a.shape, jnp.float32)
    dq_w[:, :, 0:2] = jnp.zeros((FRAMES, 8, 2, Z, C), jnp.float32)
    dq_w[:, :, 14:16] = jnp.zeros((FRAMES, 8, 2, Z, C), jnp.float32)

    def part(body, bys, hook=None):
        def frame(f, carry):
            if hook is not None:
                pl.when(f == FRAMES - 1)(hook)
            sx, sy = window_start(shifts_ref, f)

            def step(j, carry):
                for by in bys:
                    body(f, j, sx, sy, 3 * j, 2, 2 * j, by)
                for by in bys:
                    body(f, j, sx, sy, 1 + j, 4, 0, by)
                return carry

            lax.fori_loop(0, 2, step, 0)
            return carry

        lax.fori_loop(0, FRAMES, frame, 0)

    def place(nx, by):
        y0, y1 = KEYS_Y[by]
        rows = nx * (y1 - y0) * Z
        return y0, y1, rows, slice(FIRST_ROW[nx][by], FIRST_ROW[nx][by] + rows), by + (nx // 4) * 6

    def stats(f, j, sx, sy, bx, nx, kx0, by):
        y0, y1, rows, at, slot = place(nx, by)
        xq, yq = sx + 2 * bx, sy + 2 * by
        src, yo = (qgx, yq - R) if by in MID else (qgh, yq)
        qe = expanded(src, 0, xq, yo, masks)
        ge = expanded(src, 1, xq, yo, masks)
        kt = k_ref[f, pl.ds(kx0, nx), y0:y1].reshape(rows, C)
        vt = v_ref[f, pl.ds(kx0, nx), y0:y1].reshape(rows, C)
        r0 = y0 + 4 - 2 * by
        bias = bias_ref[pl.ds(kx0 + 4 - 2 * bx, nx), r0 : r0 + y1 - y0].reshape(rows, 256)
        t = (dot_t(kt, qe) + bias).reshape(rows // 8, 8, 256)
        ga = dot_t(vt, ge)
        ga_s[2 * f + j, at] = ga
        ga = ga.reshape(rows // 8, 8, 256)
        m = jnp.max(t, 0)
        m_s[2 * f + j, slot] = m
        e = jnp.exp2((t - m[None]) * C2)
        e_s[2 * f + j, at] = e.reshape(rows, 256).astype(jnp.bfloat16)
        l = jnp.sum(e, 0)
        d = jnp.sum(e * ga, 0)
        top = jnp.max(m, 0, keepdims=True)
        w = jnp.exp2((m - top) * C2)
        l = jnp.sum(l * w, 0, keepdims=True)
        d = jnp.sum(d * w, 0, keepdims=True)
        lse = top * C2 + jnp.log2(l)
        dn = d / l
        for cx in range(2):
            for val, dst in ((lse, lse_w), (dn, dn_w)):
                v2 = val[:, cx * C : (cx + 1) * C]
                other = pltpu.roll(v2, C // 2, 1)
                dst[f, 2 + 2 * bx + cx, 2 + 2 * by : 3 + 2 * by] = jnp.where(low, v2, other)
                dst[f, 2 + 2 * bx + cx, 3 + 2 * by : 4 + 2 * by] = jnp.where(low, other, v2)

    def grads(f, j, sx, sy, bx, nx, kx0, by):
        y0, y1, rows, at, slot = place(nx, by)
        xq, yq = sx + 2 * bx, sy + 2 * by
        lses, dels = [], []
        for cx in range(2):
            a = fin[xq + cx, pl.ds(yq, 1)]
            b = fin[xq + cx, pl.ds(yq + 1, 1)]
            lses.append(jnp.where(low, a, pltpu.roll(b, C // 2, 1)))
            dels.append(jnp.where(low, pltpu.roll(a, C // 2, 1), b))
        lse = jnp.concatenate(lses, 1)
        delta = jnp.concatenate(dels, 1)
        level = jnp.exp2(m_s[2 * f + j, slot] * C2 - lse)
        e = e_s[2 * f + j, at].astype(jnp.float32).reshape(rows // 8, 8, 256)
        att = (e * level[None]).reshape(rows, 256)
        gs = (att * (ga_s[2 * f + j, at] - delta)).astype(jnp.bfloat16)
        wt = att.astype(jnp.bfloat16)
        qe = expanded(qgh, 0, xq, yq, masks)
        ge = expanded(qgh, 1, xq, yq, masks)
        kt = k_ref[f, pl.ds(kx0, nx), y0:y1].reshape(rows, C)
        dk_a[f, pl.ds(kx0, nx), y0:y1] += dot_n(gs, qe).reshape(nx, y1 - y0, Z, C)
        dv_a[f, pl.ds(kx0, nx), y0:y1] += dot_n(wt, ge).reshape(nx, y1 - y0, Z, C)
        dq = dot_l(kt, gs).T
        for cx in range(2):
            for cy in range(2):
                base = (2 * cx + cy) * HEADS * Z
                out = dq[base : base + Z]
                for h in range(1, HEADS):
                    piece = dq[base + h * Z : base + (h + 1) * Z]
                    out = jnp.where(head_of_lane == h, piece, out)
                dq_w[f, 2 * bx + cx, 2 + 2 * by + cy] = out

    def frames_merged(r):
        ls, ds = [], []
        for f in range(FRAMES):
            sx, sy = window_start(shifts_ref, f)
            ls.append(lse_w[f, r + 2 - sx, pl.ds(2 - sy, 16)])
            ds.append(dn_w[f, r + 2 - sx, pl.ds(2 - sy, 16)])
        top = functools.reduce(jnp.maximum, ls)
        ws = [jnp.exp2(x - top) for x in ls]
        total = sum(ws)
        mean = sum(w * x for w, x in zip(ws, ds)) / total
        return jnp.where(low, top + jnp.log2(total), mean)

    for m in halo_x:
        m.wait_recv()
    for c in loads:
        c.wait()

    def forward_corners():
        for m in halo_y:
            m.wait_recv()
        for m in halo_c:
            m.start()

    part(stats, MID, forward_corners)
    for m in halo_c:
        m.wait_recv()

    def assemble(r, carry):
        for a in range(2):
            qgh[a, r, 0:R] = qgy[0, a, r]
            qgh[a, r, R : R + BY] = qgx[a, r]
            qgh[a, r, R + BY : HY] = qgy[1, a, r]
        return carry

    lax.fori_loop(0, HX, assemble, 0)
    part(stats, OUTER)

    def partial_rows(r, carry):
        part_s[0, r] = frames_merged(r)
        return carry

    lax.fori_loop(0, HX, partial_rows, 0)
    for m in stat_y:
        m.start()
    for m in stat_y:
        m.wait_recv()
    part_s[1, :, 0:8] = merged(part_s[0, :, 0:8], ry[0])
    part_s[1, :, 8:16] = merged(part_s[0, :, 8:16], ry[1])
    for m in stat_x:
        m.start()
    for m in stat_x:
        m.wait_recv()
    for r in range(HX):
        val = part_s[1, r]
        if r < 6:
            val = merged(val, rx1[0, r])
        if r >= 4:
            val = merged(val, rx1[1, r - 4])
        if r < 2:
            val = merged(val, rx2[0, r])
        if r >= 8:
            val = merged(val, rx2[1, r - 8])
        fin[r] = val

    part(grads, OUTER)

    def dq_sum(r, at, n):
        total = jnp.zeros((n, Z, C), jnp.float32)
        for f in range(FRAMES):
            sx, sy = window_start(shifts_ref, f)
            w = r - sx
            row = dq_w[f, jnp.clip(w, 0, 7), pl.ds(2 - sy + at, n)]
            total = total + jnp.where((w >= 0) & (w < 8), row, 0.0)
        return total * SCALE

    def dq_rims(r, carry):
        dys[0, r] = dq_sum(r, 0, R).astype(jnp.bfloat16)
        dys[1, r] = dq_sum(r, R + BY, R).astype(jnp.bfloat16)
        return carry

    lax.fori_loop(0, HX, dq_rims, 0)
    for m in dq_far:
        m.start()
    part(grads, MID)

    def dq_sides(i, carry):
        dxs[0, i] = dq_sum(i, R, BY).astype(jnp.bfloat16)
        dxs[1, i] = dq_sum(i + R + BX, R, BY).astype(jnp.bfloat16)
        return carry

    lax.fori_loop(0, R, dq_sides, 0)
    for m in dq_near:
        m.start()

    def convert(f, carry):
        k_ref[f] = (dk_a[f] * SCALE).astype(jnp.bfloat16)
        v_ref[f] = dv_a[f].astype(jnp.bfloat16)
        return carry

    lax.fori_loop(0, FRAMES, convert, 0)
    stores = [
        pltpu.make_async_copy(src, dst, out_sem.at[i])
        for i, (src, dst) in enumerate(((k_ref, dk_out), (v_ref, dv_out), (dq_v, dq_out)))
    ]
    stores[0].start()
    stores[1].start()

    def dq_core(i, carry):
        own_dq[i] = dq_sum(i + R, R, BY)
        return carry

    lax.fori_loop(0, BX, dq_core, 0)
    for m in dq_far + dq_near:
        m.wait_recv()
    rims = (slice(0, R), slice(BY - R, BY))
    for i in range(BX):
        for xs, ok, at in ((0, i < R, i), (1, i >= BX - R, i - (BX - R))):
            if ok:
                own_dq[i] += dxr[xs, at].astype(jnp.float32)
                for ys in range(2):
                    own_dq[i, rims[ys]] += dcr[xs, ys, at].astype(jnp.float32)
        for ys in range(2):
            own_dq[i, rims[ys]] += dyr[ys, i].astype(jnp.float32)
    dq_v[...] = own_dq[...].astype(jnp.bfloat16)
    stores[2].start()
    for m in made:
        m.wait_send()
    for c in stores:
        c.wait()


def per_device(saved_queries, saved_keys, saved_values, out_grad, shifts):
    bf, f32 = jnp.bfloat16, jnp.float32
    frames = saved_keys.shape
    anywhere = pl.BlockSpec(memory_space=pl.ANY)
    return pl.pallas_call(
        kernel,
        out_shape=(
            jax.ShapeDtypeStruct(saved_queries.shape, bf),
            jax.ShapeDtypeStruct(frames, bf),
            jax.ShapeDtypeStruct(frames, bf),
        ),
        in_specs=[anywhere] * 6,
        out_specs=(anywhere,) * 3,
        scratch_shapes=[
            pltpu.SMEM(shifts.shape, jnp.int32),
            pltpu.VMEM(frames, bf),
            pltpu.VMEM(frames, bf),
            pltpu.VMEM((6, 6, Z, 256), f32),
            pltpu.VMEM((2, HX, BY, Z, C), bf),
            pltpu.VMEM((2, 2, HX, R, Z, C), bf),
            pltpu.VMEM((2, HX, HY, Z, C), bf),
            pltpu.VMEM((FRAMES, 12, 24, C), f32),
            pltpu.VMEM((FRAMES, 12, 24, C), f32),
            pltpu.VMEM((2, HX, 16, C), f32),
            pltpu.VMEM((2, HX, 8, C), f32),
            pltpu.VMEM((2, 6, 16, C), f32),
            pltpu.VMEM((2, 2, 16, C), f32),
            pltpu.VMEM((HX, 16, C), f32),
            pltpu.VMEM((2 * FRAMES, ROWS, 256), bf),
            pltpu.VMEM((2 * FRAMES, ROWS, 256), f32),
            pltpu.VMEM((2 * FRAMES, 12, 8, 256), f32),
            pltpu.VMEM(frames, f32),
            pltpu.VMEM(frames, f32),
            pltpu.VMEM((FRAMES, 8, 16, Z, C), f32),
            pltpu.VMEM((2, HX, R, Z, C), bf),
            pltpu.VMEM((2, BX, R, Z, C), bf),
            pltpu.VMEM((2, 2, R, R, Z, C), bf),
            pltpu.VMEM((BX, BY, Z, C), f32),
            pltpu.VMEM((2, R, BY, Z, C), bf),
            pltpu.VMEM((2, R, BY, Z, C), bf),
            pltpu.VMEM((BX, BY, Z, C), bf),
            pltpu.SemaphoreType.DMA((6,)),
            pltpu.SemaphoreType.DMA((3,)),
            pltpu.SemaphoreType.DMA((MESSAGES,)),
            pltpu.SemaphoreType.DMA((MESSAGES,)),
        ],
        compiler_params=pltpu.CompilerParams(
            collective_id=0, has_side_effects=True, vmem_limit_bytes=60 * 2**20
        ),
    )(shifts, saved_queries, out_grad, saved_keys, saved_values, bias_table())


def solution(mesh):
    block = P("gx", "gy", None, None)
    frames = P(None, "gx", "gy", None, None)
    return jax.shard_map(
        per_device,
        mesh=mesh,
        in_specs=(block, frames, frames, block, P()),
        out_specs=(block, frames, frames),
        check_vma=False,
    )
```

```python
import functools
import math

import jax
import jax.numpy as jnp
import numpy as np
from jax import lax
from jax.experimental import pallas as pl
from jax.experimental.pallas import tpu as pltpu
from jax.sharding import PartitionSpec as P

HEADS = 4
HD = 32
C = 128
Z = 16
FRAMES = 4
R = 3
BX = 4
BY = 8
HX = BX + 2 * R
HY = BY + 2 * R
SCALE = 1.0 / math.sqrt(HD)
C2 = SCALE * math.log2(math.e)
NEG = -1e30
KEYS_Y = ((0, 2), (0, 4), (0, 6), (2, 8), (4, 8), (6, 8))


def bias_table():
    rx = np.arange(6) - 2
    col = np.arange(4)
    cx, cy = col // 2, col % 2
    okx = np.abs(rx[:, None] - cx[None]) <= 2
    oky = np.abs(rx[:, None] - cy[None]) <= 2
    z = np.arange(Z)
    okz = np.abs(z[:, None] - z[None]) <= 1
    ok = okx[:, None, None, :, None, None] & oky[None, :, None, :, None, None]
    ok = ok & okz[None, None, :, None, None, :]
    ok = np.broadcast_to(ok, (6, 6, Z, 4, HEADS, Z)).reshape(6, 6, Z, 4 * HEADS * Z)
    return jnp.asarray(np.where(ok, 0.0, NEG).astype(np.float32))


def head_masks():
    lane = lax.broadcasted_iota(jnp.int32, (Z, C), 1) // HD
    return [jnp.where(lane == h, 1.0, 0.0).astype(jnp.bfloat16) for h in range(HEADS)]


def expanded(ref, which, x, y, masks):
    parts = []
    for cx in range(2):
        for cy in range(2):
            column = ref[which, x + cx, y + cy]
            parts += [column * mask for mask in masks]
    return jnp.concatenate(parts, 0)


def dot_t(a, b):
    return lax.dot_general(a, b, (((1,), (1,)), ((), ())), preferred_element_type=jnp.float32)


def dot_n(a, b):
    return lax.dot_general(a, b, (((1,), (0,)), ((), ())), preferred_element_type=jnp.float32)


def dot_l(a, b):
    return lax.dot_general(a, b, (((0,), (0,)), ((), ())), preferred_element_type=jnp.float32)


def low_half():
    return lax.broadcasted_iota(jnp.int32, (1, C), 1) < C // 2


def window_start(shifts_ref, f):
    past = jnp.maximum(f - 1, 0)
    ox = jnp.where(f > 0, shifts_ref[0, past], 0)
    oy = jnp.where(f > 0, shifts_ref[1, past], 0)
    return 1 - ox, 1 - oy


def merged(a, b):
    low = lax.broadcasted_iota(jnp.int32, a.shape, a.ndim - 1) < C // 2
    la = jnp.where(low, a, pltpu.roll(a, C // 2, a.ndim - 1))
    lb = jnp.where(low, b, pltpu.roll(b, C // 2, b.ndim - 1))
    top = jnp.maximum(la, lb)
    wa, wb = jnp.exp2(la - top), jnp.exp2(lb - top)
    total = wa + wb
    return jnp.where(low, top + jnp.log2(total), (wa * a + wb * b) / total)


class Message:
    def __init__(self, offset, src, dst, index, sems):
        device, self.has_target, self.has_source = {}, True, True
        for axis, by in offset.items():
            at, n = lax.axis_index(axis), lax.axis_size(axis)
            device[axis] = at + by
            to, back = at + by, at - by
            self.has_target = self.has_target & (to >= 0) & (to < n)
            self.has_source = self.has_source & (back >= 0) & (back < n)
        self.copy = pltpu.make_async_remote_copy(
            src_ref=src,
            dst_ref=dst,
            send_sem=sems[0].at[index],
            recv_sem=sems[1].at[index],
            device_id=device,
            device_id_type=pl.DeviceIdType.MESH,
        )

    def start(self):
        pl.when(self.has_target)(self.copy.start)

    def wait_recv(self):
        pl.when(self.has_source)(self.copy.wait_recv)

    def wait_send(self):
        pl.when(self.has_target)(self.copy.wait_send)


PEERS = tuple(
    [{"gx": d} for d in (-2, -1, 1, 2)]
    + [{"gy": d} for d in (-1, 1)]
    + [{"gx": dx, "gy": dy} for dx in (-1, 1) for dy in (-1, 1)]
)
MID = (2, 3)
LOW = (0, 1)
HIGH = (4, 5)
RIM = 2 * R
NROWS = [2 * Z * (b - a) for a, b in KEYS_Y]
FIRST_ROW = {2: [sum(NROWS[:i]) for i in range(6)]}
FIRST_ROW[4] = [sum(NROWS) + 2 * v for v in FIRST_ROW[2]]
ROWS = 3 * sum(NROWS)
CHUNK = 64
HIGH_HOOK = 2
MESSAGES = 32


def kernel(
    shifts_in, q_in, g_in, k_in, v_in, bias_in, dq_out, dk_out, dv_out,
    shifts_ref, k_ref, v_ref, bias_ref, qgx, qgy, qgl, qgr, lse_w, dn_w, part_s, ry, rx1, rx2, fin,
    e_s, ga_s, m_s, dk_a, dv_a, dq_w, dys, dyr, dcr, own_dq, dxs, dxr, dq_v,
    local_sem, out_sem, send_sem, recv_sem,
):
    sems = (send_sem, recv_sem)
    masks = head_masks()
    low = low_half()
    head_of_lane = lax.broadcasted_iota(jnp.int32, (Z, C), 1) // HD
    loads = [
        pltpu.make_async_copy(src, dst, local_sem.at[i])
        for i, (src, dst) in enumerate(
            (
                (shifts_in, shifts_ref),
                (q_in, qgx.at[0, R : R + BX]),
                (g_in, qgx.at[1, R : R + BX]),
                (k_in, k_ref),
                (v_in, v_ref),
                (bias_in, bias_ref),
            )
        )
    ]
    for c in loads:
        c.start()

    zero16 = jnp.bfloat16(0)
    neutral = jnp.where(low, NEG, 0.0)
    for ref in (qgx.at[:, 0:R], qgx.at[:, R + BX : HX], qgy, dyr, dcr, dxr):
        ref[...] = jnp.full(ref.shape, zero16)
    for ref in (ry, rx1, rx2):
        ref[...] = jnp.broadcast_to(neutral, ref.shape)

    barrier = pltpu.get_barrier_semaphore()
    count = jnp.int32(0)
    for offset in PEERS:
        there = True
        for axis, by in offset.items():
            to = lax.axis_index(axis) + by
            there = there & (to >= 0) & (to < lax.axis_size(axis))
        device = {axis: lax.axis_index(axis) + by for axis, by in offset.items()}
        count = count + jnp.where(there, 1, 0)

        @pl.when(there)
        def _():
            pl.semaphore_signal(barrier, inc=1, device_id=device, device_id_type=pl.DeviceIdType.MESH)

    pl.semaphore_wait(barrier, count)

    made = []

    def message(offset, src, dst):
        made.append(Message(offset, src, dst, len(made), sems))
        return made[-1]

    up, down, right, left = {"gy": 1}, {"gy": -1}, {"gx": 1}, {"gx": -1}
    tail = slice(BX - R, BX)
    own = slice(R, R + BX)
    past = slice(R + BX, HX)
    halo_lo, halo_x, halo_hi = [], [], []
    for i, ref in enumerate((q_in, g_in)):
        halo_lo.append(message(up, ref.at[:, BY - R : BY], qgy.at[0, i, own]))
        halo_hi.append(message(down, ref.at[:, 0:R], qgy.at[1, i, own]))
        halo_x.append(message(right, ref.at[tail], qgx.at[i, 0:R]))
        halo_x.append(message(left, ref.at[0:R], qgx.at[i, past]))
    halo_c = [
        [
            message(right, qgy.at[side, :, BX : BX + R], qgy.at[side, :, 0:R]),
            message(left, qgy.at[side, :, R : 2 * R], qgy.at[side, :, past]),
        ]
        for side in range(2)
    ]
    stat_y = [
        message(up, part_s.at[0, :, 8:16], ry.at[0]),
        message(down, part_s.at[0, :, 0:8], ry.at[1]),
    ]
    stat_x = [
        message(right, part_s.at[1, 4:10], rx1.at[0]),
        message(left, part_s.at[1, 0:6], rx1.at[1]),
        message({"gx": 2}, part_s.at[1, 8:10], rx2.at[0]),
        message({"gx": -2}, part_s.at[1, 0:2], rx2.at[1]),
    ]
    dq_far = []
    for side, dy in ((0, -1), (1, 1)):
        ys = 1 - side
        dq_far.append(
            [
                message({"gy": dy}, dys.at[side, own], dyr.at[ys]),
                message({"gx": 1, "gy": dy}, dys.at[side, past], dcr.at[0, ys]),
                message({"gx": -1, "gy": dy}, dys.at[side, 0:R], dcr.at[1, ys]),
            ]
        )
    dq_near = [message(right, dxs.at[1], dxr.at[0]), message(left, dxs.at[0], dxr.at[1])]

    for m in halo_lo + halo_x + halo_hi:
        m.start()
    lse_w[...] = jnp.full(lse_w.shape, NEG, jnp.float32)
    dn_w[...] = jnp.zeros(dn_w.shape, jnp.float32)
    dk_a[...] = jnp.zeros(dk_a.shape, jnp.float32)
    dv_a[...] = jnp.zeros(dv_a.shape, jnp.float32)
    dq_w[:, :, 0:2] = jnp.zeros((FRAMES, 8, 2, Z, C), jnp.float32)
    dq_w[:, :, 14:16] = jnp.zeros((FRAMES, 8, 2, Z, C), jnp.float32)

    def part(body, bys, hook=None, hook_frame=FRAMES - 1):
        def frame(f, carry):
            if hook is not None:
                pl.when(f == hook_frame)(hook)
            sx, sy = window_start(shifts_ref, f)

            for by in bys:
                for j in range(2):
                    body(f, j, sx, sy, 3 * j, 2, 2 * j, by)
                    body(f, j, sx, sy, 1 + j, 4, 0, by)
            return carry

        lax.fori_loop(0, FRAMES, frame, 0, unroll=2)

    def place(nx, by):
        y0, y1 = KEYS_Y[by]
        rows = nx * (y1 - y0) * Z
        return y0, y1, rows, slice(FIRST_ROW[nx][by], FIRST_ROW[nx][by] + rows)

    def operands(xq, yq, by):
        if by in MID:
            src, yo = qgx, yq - R
        elif by in LOW:
            src, yo = qgl, yq
        else:
            src, yo = qgr, yq - BY
        return expanded(src, 0, xq, yo, masks), expanded(src, 1, xq, yo, masks)

    def stats(f, j, sx, sy, bx, nx, kx0, by):
        y0, y1, rows, at = place(nx, by)
        xq, yq = sx + 2 * bx, sy + 2 * by
        qe, ge = operands(xq, yq, by)
        kt = k_ref[f, pl.ds(kx0, nx), y0:y1].reshape(rows, C)
        vt = v_ref[f, pl.ds(kx0, nx), y0:y1].reshape(rows, C)
        r0 = y0 + 4 - 2 * by
        bias = bias_ref[pl.ds(kx0 + 4 - 2 * bx, nx), r0 : r0 + y1 - y0].reshape(rows, 256)
        t = (dot_t(kt, qe) + bias).reshape(rows // CHUNK, CHUNK // 8, 8, 256)
        ga = dot_t(vt, ge)
        ga_s[2 * f + j, at] = ga
        ga = ga.reshape(rows // CHUNK, CHUNK // 8, 8, 256)
        ms, ls, ds = [], [], []
        for i in range(rows // CHUNK):
            m = jnp.max(t[i], 0)
            e = jnp.exp2((t[i] - m[None]) * C2)
            lo = at.start + i * CHUNK
            e_s[2 * f + j, lo : lo + CHUNK] = e.reshape(CHUNK, 256).astype(jnp.bfloat16)
            m_s[2 * f + j, lo // CHUNK] = m
            ms.append(m)
            ls.append(jnp.sum(e, 0))
            ds.append(jnp.sum(e * ga[i], 0))
        top = jnp.max(functools.reduce(jnp.maximum, ms), 0, keepdims=True)
        ws = [jnp.exp2((m - top) * C2) for m in ms]
        l = jnp.sum(sum(w * x for w, x in zip(ws, ls)), 0, keepdims=True)
        d = jnp.sum(sum(w * x for w, x in zip(ws, ds)), 0, keepdims=True)
        lse = top * C2 + jnp.log2(l)
        dn = d / l
        for cx in range(2):
            for val, dst in ((lse, lse_w), (dn, dn_w)):
                v2 = val[:, cx * C : (cx + 1) * C]
                other = pltpu.roll(v2, C // 2, 1)
                dst[f, 2 + 2 * bx + cx, 2 + 2 * by : 3 + 2 * by] = jnp.where(low, v2, other)
                dst[f, 2 + 2 * bx + cx, 3 + 2 * by : 4 + 2 * by] = jnp.where(low, other, v2)

    def grads(f, j, sx, sy, bx, nx, kx0, by):
        y0, y1, rows, at = place(nx, by)
        xq, yq = sx + 2 * bx, sy + 2 * by
        lses, dels = [], []
        for cx in range(2):
            a = fin[xq + cx, pl.ds(yq, 1)]
            b = fin[xq + cx, pl.ds(yq + 1, 1)]
            lses.append(jnp.where(low, a, pltpu.roll(b, C // 2, 1)))
            dels.append(jnp.where(low, pltpu.roll(a, C // 2, 1), b))
        lse = jnp.concatenate(lses, 1)
        delta = jnp.concatenate(dels, 1)
        n = rows // CHUNK
        level = jnp.exp2(m_s[2 * f + j, at.start // CHUNK : at.start // CHUNK + n] * C2 - lse)
        e = e_s[2 * f + j, at].astype(jnp.float32).reshape(n, CHUNK // 8, 8, 256)
        att = (e * level[:, None]).reshape(rows, 256)
        gs = (att * (ga_s[2 * f + j, at] - delta)).astype(jnp.bfloat16)
        wt = att.astype(jnp.bfloat16)
        qe, ge = operands(xq, yq, by)
        kt = k_ref[f, pl.ds(kx0, nx), y0:y1].reshape(rows, C)
        dk_a[f, pl.ds(kx0, nx), y0:y1] += dot_n(gs, qe).reshape(nx, y1 - y0, Z, C)
        dv_a[f, pl.ds(kx0, nx), y0:y1] += dot_n(wt, ge).reshape(nx, y1 - y0, Z, C)
        dq = dot_l(kt, gs).T
        for cx in range(2):
            for cy in range(2):
                base = (2 * cx + cy) * HEADS * Z
                out = dq[base : base + Z]
                for h in range(1, HEADS):
                    piece = dq[base + h * Z : base + (h + 1) * Z]
                    out = jnp.where(head_of_lane == h, piece, out)
                dq_w[f, 2 * bx + cx, 2 + 2 * by + cy] = out

    def frames_merged(r, half):
        ls, ds = [], []
        for f in range(FRAMES):
            sx, sy = window_start(shifts_ref, f)
            ls.append(lse_w[f, r + 2 - sx, pl.ds(2 - sy + half.start, 8)])
            ds.append(dn_w[f, r + 2 - sx, pl.ds(2 - sy + half.start, 8)])
        top = functools.reduce(jnp.maximum, ls)
        ws = [jnp.exp2(x - top) for x in ls]
        total = sum(ws)
        mean = sum(w * x for w, x in zip(ws, ds)) / total
        return jnp.where(low, top + jnp.log2(total), mean)

    for m in halo_x:
        m.wait_recv()
    for c in loads:
        c.wait()

    def corners(side):
        for m in (halo_lo, halo_hi)[side]:
            m.wait_recv()
        for m in halo_c[side]:
            m.start()

    def assembled(side):
        for m in halo_c[side]:
            m.wait_recv()

        def row(r, carry):
            for a in range(2):
                if side == 0:
                    qgl[a, r, 0:R] = qgy[0, a, r]
                    qgl[a, r, R:RIM] = qgx[a, r, 0:R]
                else:
                    qgr[a, r, 0:R] = qgx[a, r, BY - R : BY]
                    qgr[a, r, R:RIM] = qgy[1, a, r]
            return carry

        lax.fori_loop(0, HX, row, 0)

    def partial_rows(half):
        def row(r, carry):
            part_s[0, r, half] = frames_merged(r, half)
            return carry

        lax.fori_loop(0, HX, row, 0)

    part(stats, MID, functools.partial(corners, 0))
    assembled(0)
    part(stats, LOW, functools.partial(corners, 1), HIGH_HOOK)
    partial_rows(slice(0, 8))
    stat_y[1].start()
    assembled(1)
    part(stats, HIGH)
    partial_rows(slice(8, 16))
    stat_y[0].start()
    for m in stat_y:
        m.wait_recv()
    part_s[1, :, 0:8] = merged(part_s[0, :, 0:8], ry[0])
    part_s[1, :, 8:16] = merged(part_s[0, :, 8:16], ry[1])
    for m in stat_x:
        m.start()
    for m in stat_x:
        m.wait_recv()
    for r in range(HX):
        val = part_s[1, r]
        if r < 6:
            val = merged(val, rx1[0, r])
        if r >= 4:
            val = merged(val, rx1[1, r - 4])
        if r < 2:
            val = merged(val, rx2[0, r])
        if r >= 8:
            val = merged(val, rx2[1, r - 8])
        fin[r] = val


    def dq_sum(r, at, n):
        total = jnp.zeros((n, Z, C), jnp.float32)
        for f in range(FRAMES):
            sx, sy = window_start(shifts_ref, f)
            w = r - sx
            row = dq_w[f, jnp.clip(w, 0, 7), pl.ds(2 - sy + at, n)]
            total = total + jnp.where((w >= 0) & (w < 8), row, 0.0)
        return total * SCALE

    def dq_rim(side):
        def row(r, carry):
            dys[side, r] = dq_sum(r, side * (R + BY), R).astype(jnp.bfloat16)
            return carry

        lax.fori_loop(0, HX, row, 0)
        for m in dq_far[side]:
            m.start()

    part(grads, LOW)
    dq_rim(0)
    part(grads, HIGH)
    dq_rim(1)
    part(grads, MID)

    def dq_sides(i, carry):
        dxs[0, i] = dq_sum(i, R, BY).astype(jnp.bfloat16)
        dxs[1, i] = dq_sum(i + R + BX, R, BY).astype(jnp.bfloat16)
        return carry

    lax.fori_loop(0, R, dq_sides, 0)
    for m in dq_near:
        m.start()

    def convert(f, carry):
        k_ref[f] = (dk_a[f] * SCALE).astype(jnp.bfloat16)
        v_ref[f] = dv_a[f].astype(jnp.bfloat16)
        return carry

    lax.fori_loop(0, FRAMES, convert, 0)
    stores = [
        pltpu.make_async_copy(src, dst, out_sem.at[i])
        for i, (src, dst) in enumerate(((k_ref, dk_out), (v_ref, dv_out), (dq_v, dq_out)))
    ]
    stores[0].start()
    stores[1].start()

    def dq_core(i, carry):
        own_dq[i] = dq_sum(i + R, R, BY)
        return carry

    lax.fori_loop(0, BX, dq_core, 0)
    for m in dq_far[0] + dq_far[1] + dq_near:
        m.wait_recv()
    rims = (slice(0, R), slice(BY - R, BY))
    for i in range(BX):
        for xs, ok, at in ((0, i < R, i), (1, i >= BX - R, i - (BX - R))):
            if ok:
                own_dq[i] += dxr[xs, at].astype(jnp.float32)
                for ys in range(2):
                    own_dq[i, rims[ys]] += dcr[xs, ys, at].astype(jnp.float32)
        for ys in range(2):
            own_dq[i, rims[ys]] += dyr[ys, i].astype(jnp.float32)
    dq_v[...] = own_dq[...].astype(jnp.bfloat16)
    stores[2].start()
    for m in made:
        m.wait_send()
    for c in stores:
        c.wait()


def per_device(saved_queries, saved_keys, saved_values, out_grad, shifts):
    bf, f32 = jnp.bfloat16, jnp.float32
    frames = saved_keys.shape
    anywhere = pl.BlockSpec(memory_space=pl.ANY)
    return pl.pallas_call(
        kernel,
        out_shape=(
            jax.ShapeDtypeStruct(saved_queries.shape, bf),
            jax.ShapeDtypeStruct(frames, bf),
            jax.ShapeDtypeStruct(frames, bf),
        ),
        in_specs=[anywhere] * 6,
        out_specs=(anywhere,) * 3,
        scratch_shapes=[
            pltpu.SMEM(shifts.shape[::-1], jnp.int32),
            pltpu.VMEM(frames, bf),
            pltpu.VMEM(frames, bf),
            pltpu.VMEM((6, 6, Z, 256), f32),
            pltpu.VMEM((2, HX, BY, Z, C), bf),
            pltpu.VMEM((2, 2, HX, R, Z, C), bf),
            pltpu.VMEM((2, HX, RIM, Z, C), bf),
            pltpu.VMEM((2, HX, RIM, Z, C), bf),
            pltpu.VMEM((FRAMES, 12, 24, C), f32),
            pltpu.VMEM((FRAMES, 12, 24, C), f32),
            pltpu.VMEM((2, HX, 16, C), f32),
            pltpu.VMEM((2, HX, 8, C), f32),
            pltpu.VMEM((2, 6, 16, C), f32),
            pltpu.VMEM((2, 2, 16, C), f32),
            pltpu.VMEM((HX, 16, C), f32),
            pltpu.VMEM((2 * FRAMES, ROWS, 256), bf),
            pltpu.VMEM((2 * FRAMES, ROWS, 256), f32),
            pltpu.VMEM((2 * FRAMES, ROWS // CHUNK, 8, 256), f32),
            pltpu.VMEM(frames, f32),
            pltpu.VMEM(frames, f32),
            pltpu.VMEM((FRAMES, 8, 16, Z, C), f32),
            pltpu.VMEM((2, HX, R, Z, C), bf),
            pltpu.VMEM((2, BX, R, Z, C), bf),
            pltpu.VMEM((2, 2, R, R, Z, C), bf),
            pltpu.VMEM((BX, BY, Z, C), f32),
            pltpu.VMEM((2, R, BY, Z, C), bf),
            pltpu.VMEM((2, R, BY, Z, C), bf),
            pltpu.VMEM((BX, BY, Z, C), bf),
            pltpu.SemaphoreType.DMA((6,)),
            pltpu.SemaphoreType.DMA((3,)),
            pltpu.SemaphoreType.DMA((MESSAGES,)),
            pltpu.SemaphoreType.DMA((MESSAGES,)),
        ],
        compiler_params=pltpu.CompilerParams(
            collective_id=0, has_side_effects=True, vmem_limit_bytes=60 * 2**20
        ),
    )(shifts.T, saved_queries, out_grad, saved_keys, saved_values, bias_table())


def solution(mesh):
    block = P("gx", "gy", None, None)
    frames = P(None, "gx", "gy", None, None)
    return jax.shard_map(
        per_device,
        mesh=mesh,
        in_specs=(block, frames, frames, block, P()),
        out_specs=(block, frames, frames),
        check_vma=False,
    )
```

```python
import functools
import math

import jax
import jax.numpy as jnp
import numpy as np
from jax import lax
from jax.experimental import pallas as pl
from jax.experimental.pallas import tpu as pltpu
from jax.sharding import PartitionSpec as P

HEADS = 4
HD = 32
C = 128
Z = 16
FRAMES = 4
R = 3
BX = 4
BY = 8
HX = BX + 2 * R
HY = BY + 2 * R
SCALE = 1.0 / math.sqrt(HD)
C2 = SCALE * math.log2(math.e)
NEG = -1e30
KEYS_Y = ((0, 2), (0, 4), (0, 6), (2, 8), (4, 8), (6, 8))


def bias_table():
    rx = np.arange(6) - 2
    col = np.arange(4)
    cx, cy = col // 2, col % 2
    okx = np.abs(rx[:, None] - cx[None]) <= 2
    oky = np.abs(rx[:, None] - cy[None]) <= 2
    z = np.arange(Z)
    okz = np.abs(z[:, None] - z[None]) <= 1
    ok = okx[:, None, None, :, None, None] & oky[None, :, None, :, None, None]
    ok = ok & okz[None, None, :, None, None, :]
    ok = np.broadcast_to(ok, (6, 6, Z, 4, HEADS, Z)).reshape(6, 6, Z, 4 * HEADS * Z)
    return jnp.asarray(np.where(ok, 0.0, NEG).astype(np.float32))


def head_masks():
    lane = lax.broadcasted_iota(jnp.int32, (Z, C), 1) // HD
    return [jnp.where(lane == h, 1.0, 0.0).astype(jnp.bfloat16) for h in range(HEADS)]


def expanded(ref, which, x, y, masks):
    parts = []
    for cx in range(2):
        for cy in range(2):
            column = ref[which, x + cx, y + cy]
            parts += [column * mask for mask in masks]
    return jnp.concatenate(parts, 0)


def dot_t(a, b):
    return lax.dot_general(a, b, (((1,), (1,)), ((), ())), preferred_element_type=jnp.float32)


def dot_n(a, b):
    return lax.dot_general(a, b, (((1,), (0,)), ((), ())), preferred_element_type=jnp.float32)


def dot_l(a, b):
    return lax.dot_general(a, b, (((0,), (0,)), ((), ())), preferred_element_type=jnp.float32)


def low_half():
    return lax.broadcasted_iota(jnp.int32, (1, C), 1) < C // 2


def window_start(shifts_ref, f):
    past = jnp.maximum(f - 1, 0)
    ox = jnp.where(f > 0, shifts_ref[0, past], 0)
    oy = jnp.where(f > 0, shifts_ref[1, past], 0)
    return 1 - ox, 1 - oy


def merged(a, b):
    low = lax.broadcasted_iota(jnp.int32, a.shape, a.ndim - 1) < C // 2
    la = jnp.where(low, a, pltpu.roll(a, C // 2, a.ndim - 1))
    lb = jnp.where(low, b, pltpu.roll(b, C // 2, b.ndim - 1))
    top = jnp.maximum(la, lb)
    wa, wb = jnp.exp2(la - top), jnp.exp2(lb - top)
    total = wa + wb
    return jnp.where(low, top + jnp.log2(total), (wa * a + wb * b) / total)


class Message:
    def __init__(self, offset, src, dst, index, sems):
        device, self.has_target, self.has_source = {}, True, True
        for axis, by in offset.items():
            at, n = lax.axis_index(axis), lax.axis_size(axis)
            device[axis] = at + by
            to, back = at + by, at - by
            self.has_target = self.has_target & (to >= 0) & (to < n)
            self.has_source = self.has_source & (back >= 0) & (back < n)
        self.copy = pltpu.make_async_remote_copy(
            src_ref=src,
            dst_ref=dst,
            send_sem=sems[0].at[index],
            recv_sem=sems[1].at[index],
            device_id=device,
            device_id_type=pl.DeviceIdType.MESH,
        )

    def start(self):
        pl.when(self.has_target)(self.copy.start)

    def wait_recv(self):
        pl.when(self.has_source)(self.copy.wait_recv)

    def wait_send(self):
        pl.when(self.has_target)(self.copy.wait_send)


PEERS = tuple(
    [{"gx": d} for d in (-2, -1, 1, 2)]
    + [{"gy": d} for d in (-1, 1)]
    + [{"gx": dx, "gy": dy} for dx in (-1, 1) for dy in (-1, 1)]
)
MID = (2, 3)
LOW = (0, 1)
HIGH = (4, 5)
RIM = 2 * R
NROWS = [2 * Z * (b - a) for a, b in KEYS_Y]
FIRST_ROW = {2: [sum(NROWS[:i]) for i in range(6)]}
FIRST_ROW[4] = [sum(NROWS) + 2 * v for v in FIRST_ROW[2]]
ROWS = 3 * sum(NROWS)
CHUNK = 64
HIGH_HOOK = 0
MESSAGES = 32


def kernel(
    shifts_in, q_in, g_in, k_in, v_in, bias_in, dq_out, dk_out, dv_out,
    shifts_ref, k_ref, v_ref, bias_ref, qgx, qgy, qgl, qgr, lse_w, dn_w, part_s, ry, rx1, rx2, fin,
    e_s, ga_s, m_s, dk_a, dv_a, dq_w, dys, dyr, dcr, own_dq, dxs, dxr, dq_v,
    local_sem, out_sem, send_sem, recv_sem,
):
    sems = (send_sem, recv_sem)
    masks = head_masks()
    low = low_half()
    head_of_lane = lax.broadcasted_iota(jnp.int32, (Z, C), 1) // HD
    loads = [
        pltpu.make_async_copy(src, dst, local_sem.at[i])
        for i, (src, dst) in enumerate(
            (
                (shifts_in, shifts_ref),
                (q_in, qgx.at[0, R : R + BX]),
                (g_in, qgx.at[1, R : R + BX]),
                (k_in, k_ref),
                (v_in, v_ref),
                (bias_in, bias_ref),
            )
        )
    ]
    for c in loads:
        c.start()

    zero16 = jnp.bfloat16(0)
    neutral = jnp.where(low, NEG, 0.0)
    for ref in (qgx.at[:, 0:R], qgx.at[:, R + BX : HX], qgy, dyr, dcr, dxr):
        ref[...] = jnp.full(ref.shape, zero16)
    for ref in (ry, rx1, rx2):
        ref[...] = jnp.broadcast_to(neutral, ref.shape)

    barrier = pltpu.get_barrier_semaphore()
    count = jnp.int32(0)
    for offset in PEERS:
        there = True
        for axis, by in offset.items():
            to = lax.axis_index(axis) + by
            there = there & (to >= 0) & (to < lax.axis_size(axis))
        device = {axis: lax.axis_index(axis) + by for axis, by in offset.items()}
        count = count + jnp.where(there, 1, 0)

        @pl.when(there)
        def _():
            pl.semaphore_signal(barrier, inc=1, device_id=device, device_id_type=pl.DeviceIdType.MESH)

    pl.semaphore_wait(barrier, count)

    made = []

    def message(offset, src, dst):
        made.append(Message(offset, src, dst, len(made), sems))
        return made[-1]

    up, down, right, left = {"gy": 1}, {"gy": -1}, {"gx": 1}, {"gx": -1}
    tail = slice(BX - R, BX)
    own = slice(R, R + BX)
    past = slice(R + BX, HX)
    halo_lo, halo_x, halo_hi = [], [], []
    for i, ref in enumerate((q_in, g_in)):
        halo_lo.append(message(up, ref.at[:, BY - R : BY], qgy.at[0, i, own]))
        halo_hi.append(message(down, ref.at[:, 0:R], qgy.at[1, i, own]))
        halo_x.append(message(right, ref.at[tail], qgx.at[i, 0:R]))
        halo_x.append(message(left, ref.at[0:R], qgx.at[i, past]))
    halo_c = [
        [
            message(right, qgy.at[side, :, BX : BX + R], qgy.at[side, :, 0:R]),
            message(left, qgy.at[side, :, R : 2 * R], qgy.at[side, :, past]),
        ]
        for side in range(2)
    ]
    stat_y = [
        message(up, part_s.at[0, :, 8:16], ry.at[0]),
        message(down, part_s.at[0, :, 0:8], ry.at[1]),
    ]
    stat_x = [
        message(right, part_s.at[1, 4:10], rx1.at[0]),
        message(left, part_s.at[1, 0:6], rx1.at[1]),
        message({"gx": 2}, part_s.at[1, 8:10], rx2.at[0]),
        message({"gx": -2}, part_s.at[1, 0:2], rx2.at[1]),
    ]
    dq_far = []
    for side, dy in ((0, -1), (1, 1)):
        ys = 1 - side
        dq_far.append(
            [
                message({"gy": dy}, dys.at[side, own], dyr.at[ys]),
                message({"gx": 1, "gy": dy}, dys.at[side, past], dcr.at[0, ys]),
                message({"gx": -1, "gy": dy}, dys.at[side, 0:R], dcr.at[1, ys]),
            ]
        )
    dq_near = [message(right, dxs.at[1], dxr.at[0]), message(left, dxs.at[0], dxr.at[1])]

    for m in halo_x + halo_lo + halo_hi:
        m.start()
    lse_w[...] = jnp.full(lse_w.shape, NEG, jnp.float32)
    dn_w[...] = jnp.zeros(dn_w.shape, jnp.float32)
    dk_a[...] = jnp.zeros(dk_a.shape, jnp.float32)
    dv_a[...] = jnp.zeros(dv_a.shape, jnp.float32)
    dq_w[:, :, 0:2] = jnp.zeros((FRAMES, 8, 2, Z, C), jnp.float32)
    dq_w[:, :, 14:16] = jnp.zeros((FRAMES, 8, 2, Z, C), jnp.float32)

    def part(body, bys, hook=None, hook_frame=FRAMES - 1):
        def frame(f, carry):
            if hook is not None:
                pl.when(f == hook_frame)(hook)
            sx, sy = window_start(shifts_ref, f)

            for by in bys:
                for j in range(2):
                    body(f, j, sx, sy, 3 * j, 2, 2 * j, by)
                    body(f, j, sx, sy, 1 + j, 4, 0, by)
            return carry

        lax.fori_loop(0, FRAMES, frame, 0, unroll=2)

    def place(nx, by):
        y0, y1 = KEYS_Y[by]
        rows = nx * (y1 - y0) * Z
        return y0, y1, rows, slice(FIRST_ROW[nx][by], FIRST_ROW[nx][by] + rows)

    def operands(xq, yq, by):
        if by in MID:
            src, yo = qgx, yq - R
        elif by in LOW:
            src, yo = qgl, yq
        else:
            src, yo = qgr, yq - BY
        return expanded(src, 0, xq, yo, masks), expanded(src, 1, xq, yo, masks)

    def stats(f, j, sx, sy, bx, nx, kx0, by):
        y0, y1, rows, at = place(nx, by)
        xq, yq = sx + 2 * bx, sy + 2 * by
        qe, ge = operands(xq, yq, by)
        kt = k_ref[f, pl.ds(kx0, nx), y0:y1].reshape(rows, C)
        vt = v_ref[f, pl.ds(kx0, nx), y0:y1].reshape(rows, C)
        r0 = y0 + 4 - 2 * by
        bias = bias_ref[pl.ds(kx0 + 4 - 2 * bx, nx), r0 : r0 + y1 - y0].reshape(rows, 256)
        t = (dot_t(kt, qe) + bias).reshape(rows // CHUNK, CHUNK // 8, 8, 256)
        ga = dot_t(vt, ge)
        ga_s[2 * f + j, at] = ga
        ga = ga.reshape(rows // CHUNK, CHUNK // 8, 8, 256)
        ms, ls, ds = [], [], []
        for i in range(rows // CHUNK):
            m = jnp.max(t[i], 0)
            e = jnp.exp2((t[i] - m[None]) * C2)
            lo = at.start + i * CHUNK
            e_s[2 * f + j, lo : lo + CHUNK] = e.reshape(CHUNK, 256).astype(jnp.bfloat16)
            m_s[2 * f + j, lo // CHUNK] = m
            ms.append(m)
            ls.append(jnp.sum(e, 0))
            ds.append(jnp.sum(e * ga[i], 0))
        top = jnp.max(functools.reduce(jnp.maximum, ms), 0, keepdims=True)
        ws = [jnp.exp2((m - top) * C2) for m in ms]
        l = jnp.sum(sum(w * x for w, x in zip(ws, ls)), 0, keepdims=True)
        d = jnp.sum(sum(w * x for w, x in zip(ws, ds)), 0, keepdims=True)
        lse = top * C2 + jnp.log2(l)
        dn = d / l
        for cx in range(2):
            for val, dst in ((lse, lse_w), (dn, dn_w)):
                v2 = val[:, cx * C : (cx + 1) * C]
                other = pltpu.roll(v2, C // 2, 1)
                dst[f, 2 + 2 * bx + cx, 2 + 2 * by : 3 + 2 * by] = jnp.where(low, v2, other)
                dst[f, 2 + 2 * bx + cx, 3 + 2 * by : 4 + 2 * by] = jnp.where(low, other, v2)

    def grads(f, j, sx, sy, bx, nx, kx0, by):
        y0, y1, rows, at = place(nx, by)
        xq, yq = sx + 2 * bx, sy + 2 * by
        lses, dels = [], []
        for cx in range(2):
            a = fin[xq + cx, pl.ds(yq, 1)]
            b = fin[xq + cx, pl.ds(yq + 1, 1)]
            lses.append(jnp.where(low, a, pltpu.roll(b, C // 2, 1)))
            dels.append(jnp.where(low, pltpu.roll(a, C // 2, 1), b))
        lse = jnp.concatenate(lses, 1)
        delta = jnp.concatenate(dels, 1)
        n = rows // CHUNK
        level = jnp.exp2(m_s[2 * f + j, at.start // CHUNK : at.start // CHUNK + n] * C2 - lse)
        e = e_s[2 * f + j, at].astype(jnp.float32).reshape(n, CHUNK // 8, 8, 256)
        att = (e * level[:, None]).reshape(rows, 256)
        gs = (att * (ga_s[2 * f + j, at] - delta)).astype(jnp.bfloat16)
        wt = att.astype(jnp.bfloat16)
        qe, ge = operands(xq, yq, by)
        kt = k_ref[f, pl.ds(kx0, nx), y0:y1].reshape(rows, C)
        dk_a[f, pl.ds(kx0, nx), y0:y1] += dot_n(gs, qe).reshape(nx, y1 - y0, Z, C)
        dv_a[f, pl.ds(kx0, nx), y0:y1] += dot_n(wt, ge).reshape(nx, y1 - y0, Z, C)
        dq = dot_l(kt, gs).T
        for cx in range(2):
            for cy in range(2):
                base = (2 * cx + cy) * HEADS * Z
                out = dq[base : base + Z]
                for h in range(1, HEADS):
                    piece = dq[base + h * Z : base + (h + 1) * Z]
                    out = jnp.where(head_of_lane == h, piece, out)
                dq_w[f, 2 * bx + cx, 2 + 2 * by + cy] = out

    def frames_merged(r, half):
        ls, ds = [], []
        for f in range(FRAMES):
            sx, sy = window_start(shifts_ref, f)
            ls.append(lse_w[f, r + 2 - sx, pl.ds(2 - sy + half.start, 8)])
            ds.append(dn_w[f, r + 2 - sx, pl.ds(2 - sy + half.start, 8)])
        top = functools.reduce(jnp.maximum, ls)
        ws = [jnp.exp2(x - top) for x in ls]
        total = sum(ws)
        mean = sum(w * x for w, x in zip(ws, ds)) / total
        return jnp.where(low, top + jnp.log2(total), mean)

    for m in halo_x:
        m.wait_recv()
    for c in loads:
        c.wait()

    def corners(side):
        for m in (halo_lo, halo_hi)[side]:
            m.wait_recv()
        for m in halo_c[side]:
            m.start()

    def assembled(side):
        for m in halo_c[side]:
            m.wait_recv()

        def row(r, carry):
            for a in range(2):
                if side == 0:
                    qgl[a, r, 0:R] = qgy[0, a, r]
                    qgl[a, r, R:RIM] = qgx[a, r, 0:R]
                else:
                    qgr[a, r, 0:R] = qgx[a, r, BY - R : BY]
                    qgr[a, r, R:RIM] = qgy[1, a, r]
            return carry

        lax.fori_loop(0, HX, row, 0)

    def partial_rows(half):
        def row(r, carry):
            part_s[0, r, half] = frames_merged(r, half)
            return carry

        lax.fori_loop(0, HX, row, 0)

    part(stats, MID, functools.partial(corners, 0))
    assembled(0)
    part(stats, LOW, functools.partial(corners, 1), HIGH_HOOK)
    partial_rows(slice(0, 8))
    stat_y[1].start()
    assembled(1)
    part(stats, HIGH)
    partial_rows(slice(8, 16))
    stat_y[0].start()
    for m in stat_y:
        m.wait_recv()
    part_s[1, :, 0:8] = merged(part_s[0, :, 0:8], ry[0])
    part_s[1, :, 8:16] = merged(part_s[0, :, 8:16], ry[1])
    for m in stat_x:
        m.start()
    for m in stat_x:
        m.wait_recv()
    for r in range(HX):
        val = part_s[1, r]
        if r < 6:
            val = merged(val, rx1[0, r])
        if r >= 4:
            val = merged(val, rx1[1, r - 4])
        if r < 2:
            val = merged(val, rx2[0, r])
        if r >= 8:
            val = merged(val, rx2[1, r - 8])
        fin[r] = val


    def dq_sum(r, at, n):
        total = jnp.zeros((n, Z, C), jnp.float32)
        for f in range(FRAMES):
            sx, sy = window_start(shifts_ref, f)
            w = r - sx
            row = dq_w[f, jnp.clip(w, 0, 7), pl.ds(2 - sy + at, n)]
            total = total + jnp.where((w >= 0) & (w < 8), row, 0.0)
        return total * SCALE

    def dq_rim(side):
        def row(r, carry):
            dys[side, r] = dq_sum(r, side * (R + BY), R).astype(jnp.bfloat16)
            return carry

        lax.fori_loop(0, HX, row, 0)
        for m in dq_far[side]:
            m.start()

    part(grads, LOW)
    dq_rim(0)
    part(grads, HIGH)
    dq_rim(1)
    part(grads, MID)

    def dq_sides(i, carry):
        dxs[0, i] = dq_sum(i, R, BY).astype(jnp.bfloat16)
        dxs[1, i] = dq_sum(i + R + BX, R, BY).astype(jnp.bfloat16)
        return carry

    lax.fori_loop(0, R, dq_sides, 0)
    for m in dq_near:
        m.start()

    def convert(f, carry):
        k_ref[f] = (dk_a[f] * SCALE).astype(jnp.bfloat16)
        v_ref[f] = dv_a[f].astype(jnp.bfloat16)
        return carry

    lax.fori_loop(0, FRAMES, convert, 0)
    stores = [
        pltpu.make_async_copy(src, dst, out_sem.at[i])
        for i, (src, dst) in enumerate(((k_ref, dk_out), (v_ref, dv_out), (dq_v, dq_out)))
    ]
    stores[0].start()
    stores[1].start()

    def dq_core(i, carry):
        own_dq[i] = dq_sum(i + R, R, BY)
        return carry

    lax.fori_loop(0, BX, dq_core, 0)
    for m in dq_far[0] + dq_far[1] + dq_near:
        m.wait_recv()
    rims = (slice(0, R), slice(BY - R, BY))
    for i in range(BX):
        for xs, ok, at in ((0, i < R, i), (1, i >= BX - R, i - (BX - R))):
            if ok:
                own_dq[i] += dxr[xs, at].astype(jnp.float32)
                for ys in range(2):
                    own_dq[i, rims[ys]] += dcr[xs, ys, at].astype(jnp.float32)
        for ys in range(2):
            own_dq[i, rims[ys]] += dyr[ys, i].astype(jnp.float32)
    dq_v[...] = own_dq[...].astype(jnp.bfloat16)
    stores[2].start()
    for m in made:
        m.wait_send()
    for c in stores:
        c.wait()


def hand_on(dq_in, dk_in, dv_in, dq_out, dk_out, dv_out):
    dq_out[...] = dq_in[...]
    dk_out[...] = dk_in[...]
    dv_out[...] = dv_in[...]


def per_device(saved_queries, saved_keys, saved_values, out_grad, shifts):
    bf, f32 = jnp.bfloat16, jnp.float32
    frames = saved_keys.shape
    anywhere = pl.BlockSpec(memory_space=pl.ANY)
    results = pl.pallas_call(
        kernel,
        out_shape=(
            jax.ShapeDtypeStruct(saved_queries.shape, bf),
            jax.ShapeDtypeStruct(frames, bf),
            jax.ShapeDtypeStruct(frames, bf),
        ),
        in_specs=[anywhere] * 6,
        out_specs=(anywhere,) * 3,
        scratch_shapes=[
            pltpu.SMEM(shifts.shape[::-1], jnp.int32),
            pltpu.VMEM(frames, bf),
            pltpu.VMEM(frames, bf),
            pltpu.VMEM((6, 6, Z, 256), f32),
            pltpu.VMEM((2, HX, BY, Z, C), bf),
            pltpu.VMEM((2, 2, HX, R, Z, C), bf),
            pltpu.VMEM((2, HX, RIM, Z, C), bf),
            pltpu.VMEM((2, HX, RIM, Z, C), bf),
            pltpu.VMEM((FRAMES, 12, 24, C), f32),
            pltpu.VMEM((FRAMES, 12, 24, C), f32),
            pltpu.VMEM((2, HX, 16, C), f32),
            pltpu.VMEM((2, HX, 8, C), f32),
            pltpu.VMEM((2, 6, 16, C), f32),
            pltpu.VMEM((2, 2, 16, C), f32),
            pltpu.VMEM((HX, 16, C), f32),
            pltpu.VMEM((2 * FRAMES, ROWS, 256), bf),
            pltpu.VMEM((2 * FRAMES, ROWS, 256), f32),
            pltpu.VMEM((2 * FRAMES, ROWS // CHUNK, 8, 256), f32),
            pltpu.VMEM(frames, f32),
            pltpu.VMEM(frames, f32),
            pltpu.VMEM((FRAMES, 8, 16, Z, C), f32),
            pltpu.VMEM((2, HX, R, Z, C), bf),
            pltpu.VMEM((2, BX, R, Z, C), bf),
            pltpu.VMEM((2, 2, R, R, Z, C), bf),
            pltpu.VMEM((BX, BY, Z, C), f32),
            pltpu.VMEM((2, R, BY, Z, C), bf),
            pltpu.VMEM((2, R, BY, Z, C), bf),
            pltpu.VMEM((BX, BY, Z, C), bf),
            pltpu.SemaphoreType.DMA((6,)),
            pltpu.SemaphoreType.DMA((3,)),
            pltpu.SemaphoreType.DMA((MESSAGES,)),
            pltpu.SemaphoreType.DMA((MESSAGES,)),
        ],
        compiler_params=pltpu.CompilerParams(
            collective_id=0, has_side_effects=True, vmem_limit_bytes=60 * 2**20
        ),
    )(shifts.T, saved_queries, out_grad, saved_keys, saved_values, bias_table())
    block = pl.BlockSpec((1,) + saved_queries.shape[1:], lambda i: (i, 0, 0, 0))
    frame = pl.BlockSpec((1,) + frames[1:], lambda i: (i, 0, 0, 0, 0))
    return pl.pallas_call(
        hand_on,
        out_shape=tuple(jax.ShapeDtypeStruct(r.shape, r.dtype) for r in results),
        grid=(FRAMES,),
        in_specs=[block, frame, frame],
        out_specs=(block, frame, frame),
    )(*results)


def solution(mesh):
    block = P("gx", "gy", None, None)
    frames = P(None, "gx", "gy", None, None)
    return jax.shard_map(
        per_device,
        mesh=mesh,
        in_specs=(block, frames, frames, block, P()),
        out_specs=(block, frames, frames),
        check_vma=False,
    )
```

```python
import functools
import math

import jax
import jax.numpy as jnp
import numpy as np
from jax import lax
from jax.experimental import pallas as pl
from jax.experimental.pallas import tpu as pltpu
from jax.sharding import PartitionSpec as P

HEADS = 4
HD = 32
C = 128
Z = 16
FRAMES = 4
R = 3
BX = 4
BY = 8
HX = BX + 2 * R
HY = BY + 2 * R
SCALE = 1.0 / math.sqrt(HD)
C2 = SCALE * math.log2(math.e)
NEG = -1e30
KEYS_Y = ((0, 2), (0, 4), (0, 6), (2, 8), (4, 8), (6, 8))


def bias_table():
    rx = np.arange(6) - 2
    col = np.arange(4)
    cx, cy = col // 2, col % 2
    okx = np.abs(rx[:, None] - cx[None]) <= 2
    oky = np.abs(rx[:, None] - cy[None]) <= 2
    z = np.arange(Z)
    okz = np.abs(z[:, None] - z[None]) <= 1
    ok = okx[:, None, None, :, None, None] & oky[None, :, None, :, None, None]
    ok = ok & okz[None, None, :, None, None, :]
    ok = np.broadcast_to(ok, (6, 6, Z, 4, HEADS, Z)).reshape(6, 6, Z, 4 * HEADS * Z)
    return jnp.asarray(np.where(ok, 0.0, NEG).astype(np.float32))


def head_masks():
    lane = lax.broadcasted_iota(jnp.int32, (Z, C), 1) // HD
    return [jnp.where(lane == h, 1.0, 0.0).astype(jnp.bfloat16) for h in range(HEADS)]


def expanded(ref, which, x, y, masks):
    parts = []
    for cx in range(2):
        for cy in range(2):
            column = ref[which, x + cx, y + cy]
            parts += [column * mask for mask in masks]
    return jnp.concatenate(parts, 0)


def dot_t(a, b):
    return lax.dot_general(a, b, (((1,), (1,)), ((), ())), preferred_element_type=jnp.float32)


def dot_n(a, b):
    return lax.dot_general(a, b, (((1,), (0,)), ((), ())), preferred_element_type=jnp.float32)


def dot_l(a, b):
    return lax.dot_general(a, b, (((0,), (0,)), ((), ())), preferred_element_type=jnp.float32)


def low_half():
    return lax.broadcasted_iota(jnp.int32, (1, C), 1) < C // 2


def window_start(shifts_ref, f):
    past = jnp.maximum(f - 1, 0)
    ox = jnp.where(f > 0, shifts_ref[0, past], 0)
    oy = jnp.where(f > 0, shifts_ref[1, past], 0)
    return 1 - ox, 1 - oy


def merged(a, b):
    low = lax.broadcasted_iota(jnp.int32, a.shape, a.ndim - 1) < C // 2
    la = jnp.where(low, a, pltpu.roll(a, C // 2, a.ndim - 1))
    lb = jnp.where(low, b, pltpu.roll(b, C // 2, b.ndim - 1))
    top = jnp.maximum(la, lb)
    wa, wb = jnp.exp2(la - top), jnp.exp2(lb - top)
    total = wa + wb
    return jnp.where(low, top + jnp.log2(total), (wa * a + wb * b) / total)


class Message:
    def __init__(self, offset, src, dst, index, sems):
        device, self.has_target, self.has_source = {}, True, True
        for axis, by in offset.items():
            at, n = lax.axis_index(axis), lax.axis_size(axis)
            device[axis] = at + by
            to, back = at + by, at - by
            self.has_target = self.has_target & (to >= 0) & (to < n)
            self.has_source = self.has_source & (back >= 0) & (back < n)
        self.copy = pltpu.make_async_remote_copy(
            src_ref=src,
            dst_ref=dst,
            send_sem=sems[0].at[index],
            recv_sem=sems[1].at[index],
            device_id=device,
            device_id_type=pl.DeviceIdType.MESH,
        )

    def start(self):
        pl.when(self.has_target)(self.copy.start)

    def wait_recv(self):
        pl.when(self.has_source)(self.copy.wait_recv)

    def wait_send(self):
        pl.when(self.has_target)(self.copy.wait_send)


PEERS = tuple(
    [{"gx": d} for d in (-2, -1, 1, 2)]
    + [{"gy": d} for d in (-1, 1)]
    + [{"gx": dx, "gy": dy} for dx in (-1, 1) for dy in (-1, 1)]
)
MID = (2, 3)
LOW = (0, 1)
HIGH = (4, 5)
RIM = 2 * R
NROWS = [2 * Z * (b - a) for a, b in KEYS_Y]
FIRST_ROW = {2: [sum(NROWS[:i]) for i in range(6)]}
FIRST_ROW[4] = [sum(NROWS) + 2 * v for v in FIRST_ROW[2]]
ROWS = 3 * sum(NROWS)
CHUNK = 64
HIGH_HOOK = 0
MESSAGES = 32


def kernel(
    shifts_in, q_in, g_in, k_in, v_in, bias_in, dq_out, dk_out, dv_out,
    shifts_ref, k_ref, v_ref, bias_ref, qgx, qgy, qgl, qgr, lse_w, dn_w, part_s, ry, rx1, rx2, fin,
    e_s, ga_s, m_s, dk_a, dv_a, dq_w, dys, dyr, dcr, own_dq, dxs, dxr, dq_v,
    local_sem, out_sem, send_sem, recv_sem,
):
    sems = (send_sem, recv_sem)
    masks = head_masks()
    low = low_half()
    head_of_lane = lax.broadcasted_iota(jnp.int32, (Z, C), 1) // HD
    loads = [
        pltpu.make_async_copy(src, dst, local_sem.at[i])
        for i, (src, dst) in enumerate(
            (
                (shifts_in, shifts_ref),
                (q_in, qgx.at[0, R : R + BX]),
                (g_in, qgx.at[1, R : R + BX]),
                (k_in, k_ref),
                (v_in, v_ref),
                (bias_in, bias_ref),
            )
        )
    ]
    for c in loads:
        c.start()

    zero16 = jnp.bfloat16(0)
    neutral = jnp.where(low, NEG, 0.0)
    for ref in (qgx.at[:, 0:R], qgx.at[:, R + BX : HX], qgy, dyr, dcr, dxr):
        ref[...] = jnp.full(ref.shape, zero16)
    for ref in (ry, rx1, rx2):
        ref[...] = jnp.broadcast_to(neutral, ref.shape)

    barrier = pltpu.get_barrier_semaphore()
    count = jnp.int32(0)
    for offset in PEERS:
        there = True
        for axis, by in offset.items():
            to = lax.axis_index(axis) + by
            there = there & (to >= 0) & (to < lax.axis_size(axis))
        device = {axis: lax.axis_index(axis) + by for axis, by in offset.items()}
        count = count + jnp.where(there, 1, 0)

        @pl.when(there)
        def _():
            pl.semaphore_signal(barrier, inc=1, device_id=device, device_id_type=pl.DeviceIdType.MESH)

    pl.semaphore_wait(barrier, count)

    made = []

    def message(offset, src, dst):
        made.append(Message(offset, src, dst, len(made), sems))
        return made[-1]

    up, down, right, left = {"gy": 1}, {"gy": -1}, {"gx": 1}, {"gx": -1}
    tail = slice(BX - R, BX)
    own = slice(R, R + BX)
    past = slice(R + BX, HX)
    halo_lo, halo_x, halo_hi = [], [], []
    for i, ref in enumerate((q_in, g_in)):
        halo_lo.append(message(up, ref.at[:, BY - R : BY], qgy.at[0, i, own]))
        halo_hi.append(message(down, ref.at[:, 0:R], qgy.at[1, i, own]))
        halo_x.append(message(right, ref.at[tail], qgx.at[i, 0:R]))
        halo_x.append(message(left, ref.at[0:R], qgx.at[i, past]))
    halo_c = [
        [
            message(right, qgy.at[side, :, BX : BX + R], qgy.at[side, :, 0:R]),
            message(left, qgy.at[side, :, R : 2 * R], qgy.at[side, :, past]),
        ]
        for side in range(2)
    ]
    stat_y = [
        message(up, part_s.at[0, :, 8:16], ry.at[0]),
        message(down, part_s.at[0, :, 0:8], ry.at[1]),
    ]
    stat_x = [
        message(right, part_s.at[1, 4:10], rx1.at[0]),
        message(left, part_s.at[1, 0:6], rx1.at[1]),
        message({"gx": 2}, part_s.at[1, 8:10], rx2.at[0]),
        message({"gx": -2}, part_s.at[1, 0:2], rx2.at[1]),
    ]
    dq_far = []
    for side, dy in ((0, -1), (1, 1)):
        ys = 1 - side
        dq_far.append(
            [
                message({"gy": dy}, dys.at[side, own], dyr.at[ys]),
                message({"gx": 1, "gy": dy}, dys.at[side, past], dcr.at[0, ys]),
                message({"gx": -1, "gy": dy}, dys.at[side, 0:R], dcr.at[1, ys]),
            ]
        )
    dq_near = [message(right, dxs.at[1], dxr.at[0]), message(left, dxs.at[0], dxr.at[1])]

    for m in halo_x + halo_lo + halo_hi:
        m.start()
    lse_w[...] = jnp.full(lse_w.shape, NEG, jnp.float32)
    dn_w[...] = jnp.zeros(dn_w.shape, jnp.float32)
    dk_a[...] = jnp.zeros(dk_a.shape, jnp.float32)
    dv_a[...] = jnp.zeros(dv_a.shape, jnp.float32)
    dq_w[:, :, 0:2] = jnp.zeros((FRAMES, 8, 2, Z, C), jnp.float32)
    dq_w[:, :, 14:16] = jnp.zeros((FRAMES, 8, 2, Z, C), jnp.float32)

    def part(body, bys, hook=None, hook_frame=FRAMES - 1):
        def frame(f, carry):
            if hook is not None:
                pl.when(f == hook_frame)(hook)
            sx, sy = window_start(shifts_ref, f)

            for by in bys:
                for j in range(2):
                    body(f, j, sx, sy, 3 * j, 2, 2 * j, by)
                    body(f, j, sx, sy, 1 + j, 4, 0, by)
            return carry

        lax.fori_loop(0, FRAMES, frame, 0, unroll=2)

    def place(nx, by):
        y0, y1 = KEYS_Y[by]
        rows = nx * (y1 - y0) * Z
        return y0, y1, rows, slice(FIRST_ROW[nx][by], FIRST_ROW[nx][by] + rows)

    def operands(xq, yq, by):
        if by in MID:
            src, yo = qgx, yq - R
        elif by in LOW:
            src, yo = qgl, yq
        else:
            src, yo = qgr, yq - BY
        return expanded(src, 0, xq, yo, masks), expanded(src, 1, xq, yo, masks)

    def stats(f, j, sx, sy, bx, nx, kx0, by):
        y0, y1, rows, at = place(nx, by)
        xq, yq = sx + 2 * bx, sy + 2 * by
        qe, ge = operands(xq, yq, by)
        kt = k_ref[f, pl.ds(kx0, nx), y0:y1].reshape(rows, C)
        vt = v_ref[f, pl.ds(kx0, nx), y0:y1].reshape(rows, C)
        r0 = y0 + 4 - 2 * by
        bias = bias_ref[pl.ds(kx0 + 4 - 2 * bx, nx), r0 : r0 + y1 - y0].reshape(rows, 256)
        t = (dot_t(kt, qe) + bias).reshape(rows // CHUNK, CHUNK // 8, 8, 256)
        ga = dot_t(vt, ge)
        ga_s[2 * f + j, at] = ga
        ga = ga.reshape(rows // CHUNK, CHUNK // 8, 8, 256)
        ms, ls, ds = [], [], []
        for i in range(rows // CHUNK):
            m = jnp.max(t[i], 0)
            e = jnp.exp2((t[i] - m[None]) * C2)
            lo = at.start + i * CHUNK
            e_s[2 * f + j, lo : lo + CHUNK] = e.reshape(CHUNK, 256).astype(jnp.bfloat16)
            m_s[2 * f + j, lo // CHUNK] = m
            ms.append(m)
            ls.append(jnp.sum(e, 0))
            ds.append(jnp.sum(e * ga[i], 0))
        top = jnp.max(functools.reduce(jnp.maximum, ms), 0, keepdims=True)
        ws = [jnp.exp2((m - top) * C2) for m in ms]
        l = jnp.sum(sum(w * x for w, x in zip(ws, ls)), 0, keepdims=True)
        d = jnp.sum(sum(w * x for w, x in zip(ws, ds)), 0, keepdims=True)
        lse = top * C2 + jnp.log2(l)
        dn = d / l
        for cx in range(2):
            for val, dst in ((lse, lse_w), (dn, dn_w)):
                v2 = val[:, cx * C : (cx + 1) * C]
                other = pltpu.roll(v2, C // 2, 1)
                dst[f, 2 + 2 * bx + cx, 2 + 2 * by : 3 + 2 * by] = jnp.where(low, v2, other)
                dst[f, 2 + 2 * bx + cx, 3 + 2 * by : 4 + 2 * by] = jnp.where(low, other, v2)

    def grads(f, j, sx, sy, bx, nx, kx0, by):
        y0, y1, rows, at = place(nx, by)
        xq, yq = sx + 2 * bx, sy + 2 * by
        lses, dels = [], []
        for cx in range(2):
            a = fin[xq + cx, pl.ds(yq, 1)]
            b = fin[xq + cx, pl.ds(yq + 1, 1)]
            lses.append(jnp.where(low, a, pltpu.roll(b, C // 2, 1)))
            dels.append(jnp.where(low, pltpu.roll(a, C // 2, 1), b))
        lse = jnp.concatenate(lses, 1)
        delta = jnp.concatenate(dels, 1)
        n = rows // CHUNK
        level = jnp.exp2(m_s[2 * f + j, at.start // CHUNK : at.start // CHUNK + n] * C2 - lse)
        e = e_s[2 * f + j, at].astype(jnp.float32).reshape(n, CHUNK // 8, 8, 256)
        att = (e * level[:, None]).reshape(rows, 256)
        gs = (att * (ga_s[2 * f + j, at] - delta)).astype(jnp.bfloat16)
        wt = att.astype(jnp.bfloat16)
        qe, ge = operands(xq, yq, by)
        kt = k_ref[f, pl.ds(kx0, nx), y0:y1].reshape(rows, C)
        dk_a[f, pl.ds(kx0, nx), y0:y1] += dot_n(gs, qe).reshape(nx, y1 - y0, Z, C)
        dv_a[f, pl.ds(kx0, nx), y0:y1] += dot_n(wt, ge).reshape(nx, y1 - y0, Z, C)
        dq = dot_l(kt, gs).T
        for cx in range(2):
            for cy in range(2):
                base = (2 * cx + cy) * HEADS * Z
                out = dq[base : base + Z]
                for h in range(1, HEADS):
                    piece = dq[base + h * Z : base + (h + 1) * Z]
                    out = jnp.where(head_of_lane == h, piece, out)
                dq_w[f, 2 * bx + cx, 2 + 2 * by + cy] = out

    def frames_merged(r, half):
        ls, ds = [], []
        for f in range(FRAMES):
            sx, sy = window_start(shifts_ref, f)
            ls.append(lse_w[f, r + 2 - sx, pl.ds(2 - sy + half.start, 8)])
            ds.append(dn_w[f, r + 2 - sx, pl.ds(2 - sy + half.start, 8)])
        top = functools.reduce(jnp.maximum, ls)
        ws = [jnp.exp2(x - top) for x in ls]
        total = sum(ws)
        mean = sum(w * x for w, x in zip(ws, ds)) / total
        return jnp.where(low, top + jnp.log2(total), mean)

    for m in halo_x:
        m.wait_recv()
    for c in loads:
        c.wait()

    def corners(side):
        for m in (halo_lo, halo_hi)[side]:
            m.wait_recv()
        for m in halo_c[side]:
            m.start()

    def assembled(side):
        for m in halo_c[side]:
            m.wait_recv()

        def row(r, carry):
            for a in range(2):
                if side == 0:
                    qgl[a, r, 0:R] = qgy[0, a, r]
                    qgl[a, r, R:RIM] = qgx[a, r, 0:R]
                else:
                    qgr[a, r, 0:R] = qgx[a, r, BY - R : BY]
                    qgr[a, r, R:RIM] = qgy[1, a, r]
            return carry

        lax.fori_loop(0, HX, row, 0)

    def partial_rows(half):
        def row(r, carry):
            part_s[0, r, half] = frames_merged(r, half)
            return carry

        lax.fori_loop(0, HX, row, 0)

    part(stats, MID)
    corners(0)
    corners(1)
    assembled(0)
    part(stats, LOW)
    partial_rows(slice(0, 8))
    stat_y[1].start()
    assembled(1)
    part(stats, HIGH)
    partial_rows(slice(8, 16))
    stat_y[0].start()
    for m in stat_y:
        m.wait_recv()
    part_s[1, :, 0:8] = merged(part_s[0, :, 0:8], ry[0])
    part_s[1, :, 8:16] = merged(part_s[0, :, 8:16], ry[1])
    for m in stat_x:
        m.start()
    for m in stat_x:
        m.wait_recv()
    for r in range(HX):
        val = part_s[1, r]
        if r < 6:
            val = merged(val, rx1[0, r])
        if r >= 4:
            val = merged(val, rx1[1, r - 4])
        if r < 2:
            val = merged(val, rx2[0, r])
        if r >= 8:
            val = merged(val, rx2[1, r - 8])
        fin[r] = val


    def dq_sum(r, at, n):
        total = jnp.zeros((n, Z, C), jnp.float32)
        for f in range(FRAMES):
            sx, sy = window_start(shifts_ref, f)
            w = r - sx
            row = dq_w[f, jnp.clip(w, 0, 7), pl.ds(2 - sy + at, n)]
            total = total + jnp.where((w >= 0) & (w < 8), row, 0.0)
        return total * SCALE

    def dq_rim(side):
        def row(r, carry):
            dys[side, r] = dq_sum(r, side * (R + BY), R).astype(jnp.bfloat16)
            return carry

        lax.fori_loop(0, HX, row, 0)
        for m in dq_far[side]:
            m.start()

    part(grads, LOW)
    dq_rim(0)
    part(grads, HIGH)
    dq_rim(1)
    part(grads, MID)

    def dq_sides(i, carry):
        dxs[0, i] = dq_sum(i, R, BY).astype(jnp.bfloat16)
        dxs[1, i] = dq_sum(i + R + BX, R, BY).astype(jnp.bfloat16)
        return carry

    lax.fori_loop(0, R, dq_sides, 0)
    for m in dq_near:
        m.start()

    def convert(f, carry):
        k_ref[f] = (dk_a[f] * SCALE).astype(jnp.bfloat16)
        v_ref[f] = dv_a[f].astype(jnp.bfloat16)
        return carry

    lax.fori_loop(0, FRAMES, convert, 0)
    stores = [
        pltpu.make_async_copy(src, dst, out_sem.at[i])
        for i, (src, dst) in enumerate(((k_ref, dk_out), (v_ref, dv_out), (dq_v, dq_out)))
    ]
    stores[0].start()
    stores[1].start()

    def dq_core(i, carry):
        own_dq[i] = dq_sum(i + R, R, BY)
        return carry

    lax.fori_loop(0, BX, dq_core, 0)
    for m in dq_far[0] + dq_far[1] + dq_near:
        m.wait_recv()
    rims = (slice(0, R), slice(BY - R, BY))
    for i in range(BX):
        for xs, ok, at in ((0, i < R, i), (1, i >= BX - R, i - (BX - R))):
            if ok:
                own_dq[i] += dxr[xs, at].astype(jnp.float32)
                for ys in range(2):
                    own_dq[i, rims[ys]] += dcr[xs, ys, at].astype(jnp.float32)
        for ys in range(2):
            own_dq[i, rims[ys]] += dyr[ys, i].astype(jnp.float32)
    dq_v[...] = own_dq[...].astype(jnp.bfloat16)
    stores[2].start()
    for m in made:
        m.wait_send()
    for c in stores:
        c.wait()


def hand_on(dq_in, dk_in, dv_in, dq_out, dk_out, dv_out):
    dq_out[...] = dq_in[...]
    dk_out[...] = dk_in[...]
    dv_out[...] = dv_in[...]


def per_device(saved_queries, saved_keys, saved_values, out_grad, shifts):
    bf, f32 = jnp.bfloat16, jnp.float32
    frames = saved_keys.shape
    anywhere = pl.BlockSpec(memory_space=pl.ANY)
    results = pl.pallas_call(
        kernel,
        out_shape=(
            jax.ShapeDtypeStruct(saved_queries.shape, bf),
            jax.ShapeDtypeStruct(frames, bf),
            jax.ShapeDtypeStruct(frames, bf),
        ),
        in_specs=[anywhere] * 6,
        out_specs=(anywhere,) * 3,
        scratch_shapes=[
            pltpu.SMEM(shifts.shape[::-1], jnp.int32),
            pltpu.VMEM(frames, bf),
            pltpu.VMEM(frames, bf),
            pltpu.VMEM((6, 6, Z, 256), f32),
            pltpu.VMEM((2, HX, BY, Z, C), bf),
            pltpu.VMEM((2, 2, HX, R, Z, C), bf),
            pltpu.VMEM((2, HX, RIM, Z, C), bf),
            pltpu.VMEM((2, HX, RIM, Z, C), bf),
            pltpu.VMEM((FRAMES, 12, 24, C), f32),
            pltpu.VMEM((FRAMES, 12, 24, C), f32),
            pltpu.VMEM((2, HX, 16, C), f32),
            pltpu.VMEM((2, HX, 8, C), f32),
            pltpu.VMEM((2, 6, 16, C), f32),
            pltpu.VMEM((2, 2, 16, C), f32),
            pltpu.VMEM((HX, 16, C), f32),
            pltpu.VMEM((2 * FRAMES, ROWS, 256), bf),
            pltpu.VMEM((2 * FRAMES, ROWS, 256), f32),
            pltpu.VMEM((2 * FRAMES, ROWS // CHUNK, 8, 256), f32),
            pltpu.VMEM(frames, f32),
            pltpu.VMEM(frames, f32),
            pltpu.VMEM((FRAMES, 8, 16, Z, C), f32),
            pltpu.VMEM((2, HX, R, Z, C), bf),
            pltpu.VMEM((2, BX, R, Z, C), bf),
            pltpu.VMEM((2, 2, R, R, Z, C), bf),
            pltpu.VMEM((BX, BY, Z, C), f32),
            pltpu.VMEM((2, R, BY, Z, C), bf),
            pltpu.VMEM((2, R, BY, Z, C), bf),
            pltpu.VMEM((BX, BY, Z, C), bf),
            pltpu.SemaphoreType.DMA((6,)),
            pltpu.SemaphoreType.DMA((3,)),
            pltpu.SemaphoreType.DMA((MESSAGES,)),
            pltpu.SemaphoreType.DMA((MESSAGES,)),
        ],
        compiler_params=pltpu.CompilerParams(
            collective_id=0, has_side_effects=True, vmem_limit_bytes=60 * 2**20
        ),
    )(shifts.T, saved_queries, out_grad, saved_keys, saved_values, bias_table())
    block = pl.BlockSpec((1,) + saved_queries.shape[1:], lambda i: (i, 0, 0, 0))
    frame = pl.BlockSpec((1,) + frames[1:], lambda i: (i, 0, 0, 0, 0))
    return pl.pallas_call(
        hand_on,
        out_shape=tuple(jax.ShapeDtypeStruct(r.shape, r.dtype) for r in results),
        grid=(FRAMES,),
        in_specs=[block, frame, frame],
        out_specs=(block, frame, frame),
    )(*results)


def solution(mesh):
    block = P("gx", "gy", None, None)
    frames = P(None, "gx", "gy", None, None)
    return jax.shard_map(
        per_device,
        mesh=mesh,
        in_specs=(block, frames, frames, block, P()),
        out_specs=(block, frames, frames),
        check_vma=False,
    )
```
